32 devices in a mesh: seq: 8 (over z, y), tp: 4 (over x, core).
Axes of the slice: x: 2, y: 2, z: 4, core: 2. Of those that a mesh axis runs over, the one named last changes fastest.
Arguments:
- inputs: bfloat16 [512, 8, 2048], P('seq'), may hold values from -6 to 6
- cotangent: bfloat16 [512, 8, 2048], P('seq'), may hold values from -6 to 6
- lengths: int32 [8], replicated, may hold values from 128 to 512, as said below
- norm_params: float32 [4, 2048], P(None, 'seq')
- entry_weight: float32 [2048, 3, 2048], P('seq', None, 'tp'), may hold values from -0.125 to 0.125
- entry_bias: float32 [3, 32, 64], P(None, 'tp', 'seq'), may hold values from -1.8 to 1.8
- output_weight: float32 [2048, 2048], P('seq', 'tp'), may hold values from -1 to 1
- gate_weight: float32 [2048, 2, 5632], P('seq', None, 'tp'), may hold values from -0.125 to 0.125
- down_weight: float32 [2048, 5632], P('seq', 'tp'), may hold values from -0.078125 to 0.078125
- moment_norm: float32 [4, 2048], P(None, 'seq'), may hold values from -112 to 112
- moment_entry: float32 [2048, 3, 2048], P('seq', None, 'tp'), may hold values from -48 to 48
- moment_bias: float32 [3, 32, 64], P(None, 'tp', 'seq'), may hold values from -48 to 48
- moment_output: float32 [2048, 2048], P('seq', 'tp'), may hold values from -16 to 16
- moment_gate: float32 [2048, 2, 5632], P('seq', None, 'tp'), may hold values from -10 to 10
- moment_down: float32 [2048, 5632], P('seq', 'tp'), may hold values from -20 to 20
- average_norm: float32 [4, 2048], P(None, 'seq')
- average_entry: float32 [2048, 3, 2048], P('seq', None, 'tp'), may hold values from -0.125 to 0.125
- average_bias: float32 [3, 32, 64], P(None, 'tp', 'seq'), may hold values from -1.8 to 1.8
- average_output: float32 [2048, 2048], P('seq', 'tp'), may hold values from -1 to 1
- average_gate: float32 [2048, 2, 5632], P('seq', None, 'tp'), may hold values from -0.125 to 0.125
- average_down: float32 [2048, 5632], P('seq', 'tp'), may hold values from -0.078125 to 0.078125
Outputs:
- layer_out: bfloat16 [512, 8, 2048], P('seq')
- input_grad: bfloat16 [512, 8, 2048], P('seq')
- momentum_norm: float32 [4, 2048], P(None, 'seq')
- momentum_entry: float32 [2048, 3, 2048], P('seq', None, 'tp')
- momentum_bias: float32 [3, 32, 64], P(None, 'tp', 'seq')
- momentum_output: float32 [2048, 2048], P('seq', 'tp')
- momentum_gate: float32 [2048, 2, 5632], P('seq', None, 'tp')
- momentum_down: float32 [2048, 5632], P('seq', 'tp')
- weight_norm: float32 [4, 2048], P(None, 'seq')
- weight_entry: float32 [2048, 3, 2048], P('seq', None, 'tp')
- weight_bias: float32 [3, 32, 64], P(None, 'tp', 'seq')
- weight_output: float32 [2048, 2048], P('seq', 'tp')
- weight_gate: float32 [2048, 2, 5632], P('seq', None, 'tp')
- weight_down: float32 [2048, 5632], P('seq', 'tp')
- smooth_norm: float32 [4, 2048], P(None, 'seq')
- smooth_entry: float32 [2048, 3, 2048], P('seq', None, 'tp')
- smooth_bias: float32 [3, 32, 64], P(None, 'tp', 'seq')
- smooth_output: float32 [2048, 2048], P('seq', 'tp')
- smooth_gate: float32 [2048, 2, 5632], P('seq', None, 'tp')
- smooth_down: float32 [2048, 5632], P('seq', 'tp')
- copy_norm: bfloat16 [4, 2048], P(None, 'seq')
- copy_entry: bfloat16 [2048, 3, 2048], P('seq', None, 'tp')
- copy_bias: bfloat16 [3, 32, 64], P(None, 'tp', 'seq')
- copy_output: bfloat16 [2048, 2048], P('seq', 'tp')
- copy_gate: bfloat16 [2048, 2, 5632], P('seq', None, 'tp')
- copy_down: bfloat16 [2048, 5632], P('seq', 'tp')
The draws below stay inside these ranges and needn't reach their ends.
Inputs may be any that keep to these rules, and one draw needn't show every extreme that they name: `lengths`: in each micro-batch of 4 rows, at least one row is 512 tokens long.
All inputs are finite; a program needn't handle non-finite values.
Results may differ from the reference program's by a relative error of at most 0.025.
Values may be sent and summed in bfloat16 or wider, within the bound.
No kernel may reach another device: no remote copies, remote signals or barrier semaphores. Data moves between devices by JAX's collectives and lax.ppermute only.
A program may use at most 192 MiB of HBM per device.

```python
import jax
import jax.numpy as jnp
from jax import lax

D = 2048
HEADS = 32
HD = 64
FF = 5632
ROT = 16
ROWS_MB = 4
MICRO = 2
STEP = 10
ROWS = 8
LENGTH = 512


def norm_rows(key, shape):
    gains = 1.0 + 0.1 * jax.random.truncated_normal(key, -3.0, 3.0, shape)
    shifts = 0.2 * jax.random.truncated_normal(jax.random.fold_in(key, 1), -3.0, 3.0, shape)
    rows = jnp.arange(shape[0])[:, None]
    return jnp.where(rows % 2 == 0, gains, shifts).astype(jnp.float32)


def draw_lengths(key, part):
    key = jax.random.fold_in(key, 11)
    first, second = jax.random.split(key)
    values = jax.random.randint(first, (ROWS,), LENGTH // 4, LENGTH + 1)
    chosen = jax.random.randint(second, (MICRO,), 0, ROWS_MB)
    rows = jnp.arange(ROWS)
    full = rows % ROWS_MB == chosen[rows // ROWS_MB]
    return jnp.where(full, LENGTH, values).astype(jnp.int32)


def draw_norm_params(key, part):
    key = jax.random.fold_in(key, 23)
    return norm_rows(key, (4, D))


def draw_average_norm(key, part):
    key = jax.random.fold_in(key, 37)
    return norm_rows(key, (4, D))


def block_levels(key, dims, cuts, low, high):
    loudness = 1.0
    for dim, shards_of in cuts:
        heights = jax.random.uniform(jax.random.fold_in(jax.random.fold_in(key, 6), dim), (shards_of,), jnp.float32, low / len(cuts), high / len(cuts))
        loudness = loudness * jnp.repeat(jnp.exp(heights), dims[dim] // shards_of).reshape((-1,) + (1,) * (len(dims) - 1 - dim))
    return loudness


def bell_draw(own_key, extent, deviation, most, cuts=(), kind=jnp.bfloat16):
    loudness = block_levels(own_key, extent, cuts, -0.22, 0.18) if cuts else 1.0
    array = jax.random.normal(own_key, extent, jnp.float32) * deviation * loudness
    return jnp.minimum(jnp.maximum(array, -most), most).astype(kind)


def setup_inputs(seed: int = 0) -> dict:
    key_of = jax.random.split(jax.random.key(seed), 22)
    inputs = bell_draw(key_of[0], (LENGTH, ROWS, D), 1.0, 6.0, ((0, 8),))
    cotangent = bell_draw(key_of[1], (LENGTH, ROWS, D), 1.0, 6.0, ((0, 8),))
    lengths = draw_lengths(jax.random.fold_in(key_of[21], 71), 0)
    norm_params = draw_norm_params(jax.random.fold_in(key_of[21], 71), 0)
    entry_weight = bell_draw(key_of[4], (D, 3, HEADS * HD), D ** -0.5, 0.125, ((0, 8), (2, 4)), jnp.float32)
    entry_bias = bell_draw(key_of[5], (3, HEADS, HD), 0.3, 1.8, ((1, 4), (2, 8)), jnp.float32)
    output_weight = bell_draw(key_of[6], (D, HEADS * HD), (HEADS * HD // 64) ** -0.5, 1.0, ((0, 8), (1, 4)), jnp.float32)
    gate_weight = bell_draw(key_of[7], (D, 2, FF), D ** -0.5, 0.125, ((0, 8), (2, 4)), jnp.float32)
    down_weight = bell_draw(key_of[8], (D, FF), FF ** -0.5, 0.078125, ((0, 8), (1, 4)), jnp.float32)
    moment_norm = bell_draw(key_of[9], (4, D), (0.3 * (ROWS * LENGTH) ** 0.5), 112.0, ((1, 8),), jnp.float32)
    moment_entry = bell_draw(key_of[10], (D, 3, HEADS * HD), (0.12 * (ROWS * LENGTH) ** 0.5), 48.0, ((0, 8), (2, 4)), jnp.float32)
    moment_bias = bell_draw(key_of[11], (3, HEADS, HD), (0.12 * (ROWS * LENGTH) ** 0.5), 48.0, ((1, 4), (2, 8)), jnp.float32)
    moment_output = bell_draw(key_of[12], (D, HEADS * HD), (0.04 * (ROWS * LENGTH) ** 0.5), 16.0, ((0, 8), (1, 4)), jnp.float32)
    moment_gate = bell_draw(key_of[13], (D, 2, FF), (0.025 * (ROWS * LENGTH) ** 0.5), 10.0, ((0, 8), (2, 4)), jnp.float32)
    moment_down = bell_draw(key_of[14], (D, FF), (0.05 * (ROWS * LENGTH) ** 0.5), 20.0, ((0, 8), (1, 4)), jnp.float32)
    average_norm = draw_average_norm(jax.random.fold_in(key_of[21], 71), 0)
    average_entry = bell_draw(key_of[16], (D, 3, HEADS * HD), D ** -0.5, 0.125, ((0, 8), (2, 4)), jnp.float32)
    average_bias = bell_draw(key_of[17], (3, HEADS, HD), 0.3, 1.8, ((1, 4), (2, 8)), jnp.float32)
    average_output = bell_draw(key_of[18], (D, HEADS * HD), (HEADS * HD // 64) ** -0.5, 1.0, ((0, 8), (1, 4)), jnp.float32)
    average_gate = bell_draw(key_of[19], (D, 2, FF), D ** -0.5, 0.125, ((0, 8), (2, 4)), jnp.float32)
    average_down = bell_draw(key_of[20], (D, FF), FF ** -0.5, 0.078125, ((0, 8), (1, 4)), jnp.float32)
    return dict(inputs=inputs, cotangent=cotangent, lengths=lengths, norm_params=norm_params, entry_weight=entry_weight, entry_bias=entry_bias, output_weight=output_weight, gate_weight=gate_weight, down_weight=down_weight, moment_norm=moment_norm, moment_entry=moment_entry, moment_bias=moment_bias, moment_output=moment_output, moment_gate=moment_gate, moment_down=moment_down, average_norm=average_norm, average_entry=average_entry, average_bias=average_bias, average_output=average_output, average_gate=average_gate, average_down=average_down)


eps = 1e-05
rates = (0.0005, 0.0002, 0.0025, 0.004, 0.0002, 6e-05)
decays = (0.0, 0.0001, 0.0, 0.0001, 0.0001, 0.0001)
highest = lax.Precision.HIGHEST

@jax.custom_vjp
def low(v):
    return lax.optimization_barrier(v.astype(jnp.bfloat16)).astype(jnp.float32)

@jax.custom_vjp
def low_back(v):
    return v

def low_keep(v):
    return (low(v), None)

def low_pass(kept, grad):
    return (grad,)

def back_keep(v):
    return (v, None)

def back_low(kept, grad):
    return (low(grad),)
low.defvjp(low_keep, low_pass)
low_back.defvjp(back_keep, back_low)

def layer_norm(values, gain, shift):
    center = values - lax.optimization_barrier(jnp.mean(values, -1, keepdims=True))
    var = lax.optimization_barrier(jnp.mean(center * center, -1, keepdims=True))
    return center * lax.rsqrt(var + eps) * gain + shift

def turning(positions):
    half = ROT // 2
    freq = 10000.0 ** (-jnp.arange(half).astype(jnp.float32) / half)
    angle = positions.astype(jnp.float32)[:, None] * freq[None, :]
    return (jnp.cos(angle)[:, None, None, :], jnp.sin(angle)[:, None, None, :])

def rotate(values, cosine, sine):
    half = ROT // 2
    first = values[..., :half]
    second = values[..., half:ROT]
    return jnp.concatenate([first * cosine - second * sine, second * cosine + first * sine, values[..., ROT:]], -1)

def attend_row(args):
    query, keys, vals, length = args
    total = query.shape[0]
    block = min(512, total)
    starts = jnp.arange(total // block) * block
    pieces = query.reshape(total // block, block, HEADS, HD)

    def one_block(item):
        piece, first = item
        scores = low_back(jnp.einsum('qhd,khd->hqk', piece, keys, precision=highest))
        qpos = first + jnp.arange(block)
        kpos = jnp.arange(total)
        valid = (kpos[None, :] <= qpos[:, None]) & (kpos[None, :] < length)
        masked = jnp.where(valid[None], scores, -1e+30)
        top = lax.optimization_barrier(jnp.max(masked, -1, keepdims=True))
        weights = jnp.where(valid[None], jnp.exp(masked - top), 0.0)
        probs = weights / lax.optimization_barrier(jnp.sum(weights, -1, keepdims=True))
        return jnp.einsum('hqk,khd->qhd', low(probs), vals, precision=highest)
    result = lax.map(jax.checkpoint(one_block), (pieces, starts))
    return result.reshape(total, HEADS, HD)

def forward(values, lengths, params):
    w_norm, w_entry, b_entry, w_output, w_gate, w_down = params
    total, batch, width = values.shape
    h_first = layer_norm(values, w_norm[0], w_norm[1])
    a_first = low(h_first)
    mixed = jnp.einsum('lrd,dcf->lrcf', a_first, w_entry, precision=highest) + b_entry.reshape(3, HEADS * HD)
    mixed = low_back(mixed)
    heads = mixed.reshape(total, batch, 3, HEADS, HD)
    cosine, sine = turning(jnp.arange(total))
    query = low(rotate(heads[:, :, 0], cosine, sine) * 0.125)
    keys = low(rotate(heads[:, :, 1], cosine, sine))
    vals = low(heads[:, :, 2])
    attended = lax.map(attend_row, (jnp.swapaxes(query, 0, 1), jnp.swapaxes(keys, 0, 1), jnp.swapaxes(vals, 0, 1), lengths))
    attended = jnp.swapaxes(attended, 0, 1).reshape(total, batch, HEADS * HD)
    att = low(low_back(attended))
    second = values + low_back(jnp.einsum('lrh,dh->lrd', att, w_output, precision=highest))
    a_second = low(layer_norm(second, w_norm[2], w_norm[3]))
    gated = low_back(jnp.einsum('lrd,dgf->lrgf', a_second, w_gate, precision=highest))
    hidden = low(low_back(jax.nn.silu(gated[:, :, 0]) * gated[:, :, 1]))
    return second + jnp.einsum('lrf,df->lrd', hidden, w_down, precision=highest)

def reference(inputs, cotangent, lengths, norm_params, entry_weight, entry_bias, output_weight, gate_weight, down_weight, moment_norm, moment_entry, moment_bias, moment_output, moment_gate, moment_down, average_norm, average_entry, average_bias, average_output, average_gate, average_down):
    masters = (norm_params, entry_weight, entry_bias, output_weight, gate_weight, down_weight)
    moments = (moment_norm, moment_entry, moment_bias, moment_output, moment_gate, moment_down)
    averages = (average_norm, average_entry, average_bias, average_output, average_gate, average_down)
    params = tuple((low(w) for w in masters))
    values = inputs.astype(jnp.float32)
    real = jnp.arange(LENGTH)[:, None] < lengths[None, :]
    start_grad = jnp.where(real[:, :, None], cotangent.astype(jnp.float32), 0.0)
    output, pullback = jax.vjp(lambda v, p: forward(v, lengths, p), values, params)
    dvalues, dparams = pullback(start_grad)
    beta = min(0.999, (1 + STEP) / (10 + STEP))
    news, weights, smooths, copies = ([], [], [], [])
    for index in range(6):
        grad = dparams[index] + decays[index] * masters[index]
        moment = 0.9 * moments[index] + grad
        weight = masters[index] - rates[index] * (grad + 0.9 * moment)
        news.append(moment)
        weights.append(weight)
        smooths.append(beta * averages[index] + (1.0 - beta) * weight)
        copies.append(weight.astype(jnp.bfloat16))
    return (output.astype(jnp.bfloat16), dvalues.astype(jnp.bfloat16), news[0], news[1], news[2], news[3], news[4], news[5], weights[0], weights[1], weights[2], weights[3], weights[4], weights[5], smooths[0], smooths[1], smooths[2], smooths[3], smooths[4], smooths[5], copies[0], copies[1], copies[2], copies[3], copies[4], copies[5])
```

```python
import numpy as np

import jax
import jax.numpy as jnp
from jax import lax
from jax.sharding import PartitionSpec as P

HD = 64
ROT = 16
STEP = 10

eps = 1e-05
rates = (0.0005, 0.0002, 0.0025, 0.004, 0.0002, 6e-05)
decays = (0.0, 0.0001, 0.0, 0.0001, 0.0001, 0.0001)
bf16 = jnp.bfloat16
f32 = jnp.float32


def swap(array, axis, mask):
    pairs = [(i, i ^ mask) for i in range(lax.axis_size(axis))]
    return lax.ppermute(array, axis, pairs)


def pick(parts, flags):
    count = len(parts)
    for place, flag in enumerate(flags):
        bit = count >> (place + 1)
        parts = [jnp.where(flag, parts[j ^ bit], parts[j]) for j in range(count)]
    return parts


def joined(parts, axis=0):
    return parts[0] if len(parts) == 1 else jnp.concatenate(parts, axis)


def gather(piece, steps):
    pieces = {0: piece}
    rows = piece.shape[0]
    for axis, mask, bit in steps:
        keys = sorted(pieces)
        got = swap(joined([pieces[k] for k in keys]), axis, mask)
        for place, k in enumerate(keys):
            pieces[k | bit] = got[place * rows : (place + 1) * rows]
    return pieces


def scatter(pieces, steps):
    for axis, mask, bit in steps:
        keys = sorted(k for k in pieces if k & bit)
        got = swap(joined([pieces[k].astype(bf16) for k in keys]), axis, mask)
        rows = got.shape[0] // len(keys)
        kept = {k: v for k, v in pieces.items() if not k & bit}
        for place, k in enumerate(keys):
            kept[k ^ bit] = kept[k ^ bit].astype(f32) + got[place * rows : (place + 1) * rows].astype(f32)
        pieces = kept
    return pieces[0]


class Plan:
    def __init__(self, rows):
        self.n_seq = lax.axis_size("seq")
        self.n_tp = lax.axis_size("tp")
        self.seq = lax.axis_index("seq")
        self.tp = lax.axis_index("tp")
        bits = self.n_seq.bit_length() - 1
        self.inner = [2 << i for i in range(bits // 2)][::-1]
        self.outer = [1 << i for i in range(bits) if (1 << i) not in self.inner]
        self.groups = 1 << len(self.outer)
        self.parts = 1 << len(self.inner)
        self.rows = rows // self.groups
        self.group_flags = [(self.seq & m) != 0 for m in self.outer]
        self.part_flags = [(self.seq & m) != 0 for m in self.inner]
        self.tp_masks = [1 << i for i in range(self.n_tp.bit_length() - 1)]
        self.tp_flags = [(self.tp & m) != 0 for m in self.tp_masks[::-1]]
        self.group = self.index(self.group_flags)
        order = [("tp", m) for m in self.tp_masks] + [("seq", m) for m in self.inner]
        self.members = 1 << len(order)
        self.steps = [(axis, mask, self.members >> (i + 1)) for i, (axis, mask) in enumerate(order)]
        self.group_steps = [("seq", m, self.groups >> (i + 1)) for i, m in enumerate(self.outer)]

    def index(self, flags):
        value = jnp.int32(0)
        for flag in flags:
            value = value * 2 + flag.astype(jnp.int32)
        return value

    def outer_mask(self, j):
        return sum(m for i, m in enumerate(self.outer) if j & (self.groups >> (i + 1)))

    def inner_mask(self, j):
        return sum(m for i, m in enumerate(self.inner) if j & (self.parts >> (i + 1)))

    def member_masks(self, k):
        seq = sum(m for a, m, bit in self.steps if a == "seq" and k & bit)
        tp = sum(m for a, m, bit in self.steps if a == "tp" and k & bit)
        return seq, tp

    def arranged(self, array):
        wide = array.shape[-1] // self.n_seq
        sets = []
        for g in range(self.groups):
            places = [self.outer_mask(g) | self.inner_mask(h) for h in range(self.parts)]
            sets.append(joined([array[..., p * wide : (p + 1) * wide] for p in places], -1))
        return joined(pick(sets, self.group_flags), -1)

    def restored(self, array):
        wide = array.shape[-1] // self.groups
        sets = pick([array[..., g * wide : (g + 1) * wide] for g in range(self.groups)], self.group_flags)
        block = wide // self.parts
        blocks = [None] * self.n_seq
        for g in range(self.groups):
            for h in range(self.parts):
                blocks[self.outer_mask(g) | self.inner_mask(h)] = sets[g][..., h * block : (h + 1) * block]
        return joined(blocks, -1)

    def inputs_of_rows(self, array):
        part = array.shape[0] // self.n_tp
        own = lax.dynamic_slice_in_dim(array, self.tp * part, part, 0)
        got = []
        for j in range(self.groups):
            piece = lax.dynamic_slice_in_dim(own, (self.group ^ j) * self.rows, self.rows, 1)
            got.append(swap(piece, "seq", self.outer_mask(j)) if j else piece)
        stacked = jnp.swapaxes(jnp.concatenate(got, 0), 0, 1)
        return self.arranged(stacked.reshape(-1, array.shape[2]))

    def outputs_of_rows(self, tokens, part):
        width = tokens.shape[-1]
        table = self.restored(tokens).reshape(self.rows, self.groups, part, width)
        got = []
        for j in range(self.groups):
            piece = jnp.swapaxes(table[:, j], 0, 1)
            got.append(swap(piece, "seq", self.outer_mask(j)) if j else piece)
        own = joined(pick(got, self.group_flags), 1)
        steps = [("tp", m, m) for m in self.tp_masks[::-1]]
        pieces = gather(own, steps)
        return joined(pick([pieces[k] for k in range(self.n_tp)], self.tp_flags), 0)

    def gather_tokens(self, piece):
        half = piece.shape[0] // 2
        far = self.steps[1:]
        first = gather(piece[:half], far[::-1])
        second = gather(piece[half:], far)
        chips = 1 << len(far)
        near = joined([x for k in range(chips) for x in (first[k], second[k])])
        axis, mask, _ = self.steps[0]
        return jnp.concatenate([near, swap(near, axis, mask)], 0)

    def sum_tokens(self, product):
        total = self.total
        half = total // 2
        axis, mask, _ = self.steps[0]
        got = swap(product(half, total).astype(bf16), axis, mask)
        near = product(0, half) + got.astype(f32)
        far = self.steps[1:]
        chips = 1 << len(far)
        rows = half // chips
        first = {k: near[k * rows : k * rows + rows // 2] for k in range(chips)}
        second = {k: near[k * rows + rows // 2 : (k + 1) * rows] for k in range(chips)}
        return jnp.concatenate([scatter(first, far), scatter(second, far[::-1])], 0)

    def spread_weight(self, parts):
        mine = pick(parts, self.part_flags)
        got = [mine[0]] + [swap(mine[j], "seq", self.inner_mask(j)) for j in range(1, self.parts)]
        block = joined(pick(got, self.part_flags), 0)
        pieces = {0: block}
        for axis, mask, bit in self.group_steps[::-1]:
            for k in sorted(pieces):
                pieces[k | bit] = swap(pieces[k], axis, mask)
        return joined([pieces[k] for k in range(self.groups)], 0)

    def collect_grad(self, left, right, axis=-1):
        width = left.shape[1]
        block = width // self.groups
        half = width // 2

        def product(lo, hi):
            return jnp.einsum("td,tf->df", left[:, lo:hi], right, preferred_element_type=f32)

        axis_name, mask, _ = self.group_steps[0]
        got = swap(product(half, width).astype(bf16), axis_name, mask)
        kept = product(0, half) + got.astype(f32)
        pieces = {j: kept[j * block : (j + 1) * block] for j in range(self.groups // 2)}
        block_sum = scatter(pieces, self.group_steps[1:])
        rows = block // self.parts
        blocks = [block_sum[h * rows : (h + 1) * rows] for h in range(self.parts)]
        mine = pick(blocks, self.part_flags)
        got = [mine[0]] + [
            swap(mine[j].astype(bf16), "seq", self.inner_mask(j)).astype(f32) for j in range(1, self.parts)
        ]
        return pick(got, self.part_flags)


def layer_norm(values, gain, shift):
    center = values - jnp.mean(values, -1, keepdims=True)
    var = jnp.mean(center * center, -1, keepdims=True)
    inverse = lax.rsqrt(var + eps)
    normed = center * inverse
    return (normed * gain + shift, normed, inverse)


def norm_back(grad, normed, inverse, gain):
    scaled = grad * gain
    inner = (
        scaled
        - jnp.mean(scaled, -1, keepdims=True)
        - normed * jnp.mean(scaled * normed, -1, keepdims=True)
    )
    return inner * inverse


def turning(positions):
    half = ROT // 2
    freq = 10000.0 ** (-jnp.arange(half).astype(f32) / half)
    angle = positions.astype(f32)[:, None] * freq[None, :]
    return (jnp.cos(angle)[:, None, :], jnp.sin(angle)[:, None, :])


def rotate(values, cosine, sine):
    half = ROT // 2
    first = values[..., :half]
    second = values[..., half:ROT]
    return jnp.concatenate(
        [first * cosine - second * sine, second * cosine + first * sine, values[..., ROT:]], -1
    )


def body(
    inputs,
    cotangent,
    lengths,
    norm_params,
    entry_weight,
    entry_bias,
    output_weight,
    gate_weight,
    down_weight,
    moment_norm,
    moment_entry,
    moment_bias,
    moment_output,
    moment_gate,
    moment_down,
    average_norm,
    average_entry,
    average_bias,
    average_output,
    average_gate,
    average_down,
):
    plan = Plan(inputs.shape[1])
    groups, parts, rows = plan.groups, plan.parts, plan.rows
    block_len, _, width = inputs.shape
    tp_width = entry_weight.shape[2]
    head_width = tp_width // parts
    heads_here = head_width // HD
    hidden = gate_weight.shape[2] // parts
    quarter = block_len // plan.n_tp
    share = rows * groups * quarter
    plan.total = share * plan.members
    length = block_len * plan.n_seq

    member_seq = np.array([plan.member_masks(k)[0] for k in range(plan.members)], np.int32)
    member_tp = np.array([plan.member_masks(k)[1] for k in range(plan.members)], np.int32)
    sender = np.array([plan.outer_mask(j) for j in range(groups)], np.int32)
    seq_at = plan.seq ^ (member_seq[:, None] | sender[None, :])
    tp_at = plan.tp ^ member_tp
    position = (
        (seq_at * block_len)[:, :, None]
        + (tp_at * quarter)[:, None, None]
        + np.arange(quarter, dtype=np.int32)[None, None, :]
    )
    row_position = position.reshape(length)
    own_position = position[0].reshape(groups * quarter)
    lens = lax.dynamic_slice_in_dim(lengths, plan.group * rows, rows, 0)

    packed = jnp.concatenate([norm_params.reshape(-1), entry_bias.reshape(-1)]).astype(bf16)
    small = gather(packed[None], plan.group_steps[::-1])
    small = jnp.concatenate([small[j] for j in range(groups)], 0)[None]
    got = [small] + [swap(small, "seq", plan.inner_mask(h)) for h in range(1, parts)]
    small = jnp.stack(pick([g[0] for g in got], plan.part_flags), 1)
    n_norm = norm_params.size
    w_norm = small[:, :, :n_norm].reshape(groups, parts, 4, -1)
    gains = jnp.transpose(w_norm, (2, 0, 1, 3)).reshape(4, width).astype(f32)
    b_all = small[:, :, n_norm:].reshape((groups * parts,) + entry_bias.shape)
    b_all = pick([b_all[g * parts : (g + 1) * parts] for g in range(groups)], plan.group_flags)
    ordered = [None] * plan.n_seq
    for g in range(groups):
        for h in range(parts):
            ordered[plan.outer_mask(g) | plan.inner_mask(h)] = b_all[g][h]
    b_entry = jnp.concatenate(ordered, -1)
    part_at = plan.index(plan.part_flags)
    b_entry = lax.dynamic_slice_in_dim(b_entry, part_at * heads_here, heads_here, 1)
    entry_shift = b_entry.astype(f32).reshape(3 * head_width)

    def columns(array, h, size):
        return array[..., h * size : (h + 1) * size].astype(bf16).reshape(array.shape[0], -1)

    resid = plan.inputs_of_rows(inputs).astype(f32)
    w_attn = plan.spread_weight(
        [
            jnp.concatenate(
                [columns(entry_weight, h, head_width), columns(output_weight, h, head_width)], 1
            )
            for h in range(parts)
        ]
    )
    w_gate = plan.spread_weight([columns(gate_weight, h, hidden) for h in range(parts)])
    w_down = plan.spread_weight([columns(down_weight, h, hidden) for h in range(parts)])
    w_entry = w_attn[:, : 3 * head_width]
    w_output = w_attn[:, 3 * head_width :]

    h_first, n_first, i_first = layer_norm(resid, gains[0], gains[1])
    a_first = plan.gather_tokens(h_first.astype(bf16))
    mixed = jnp.einsum("td,df->tf", a_first, w_entry, preferred_element_type=f32) + entry_shift
    heads = mixed.reshape(plan.members, rows, groups * quarter, 3, heads_here, HD)
    heads = jnp.swapaxes(heads, 0, 1).reshape(rows, length, 3, heads_here, HD)
    cosine, sine = turning(row_position)
    query = (rotate(heads[:, :, 0], cosine, sine) * 0.125).astype(bf16)
    keys = rotate(heads[:, :, 1], cosine, sine).astype(bf16)
    vals = heads[:, :, 2].astype(bf16)
    valid = (row_position[None, :] <= row_position[:, None])[None, None] & (
        row_position[None, None, None, :] < lens[:, None, None, None]
    )
    scores = jnp.einsum("rqhd,rkhd->rhqk", query, keys, preferred_element_type=f32)
    scores = jnp.where(valid, scores, -1e30)
    top = jnp.max(scores, -1)
    weights = jnp.where(valid, jnp.exp(scores - top[..., None]), 0.0)
    total = jnp.sum(weights, -1)
    probs = weights / total[..., None]
    attended = jnp.einsum("rhqk,rkhd->rqhd", probs.astype(bf16), vals, preferred_element_type=f32)

    def by_member(array):
        wide = array.shape[2:]
        array = array.reshape((rows, plan.members, groups * quarter) + wide)
        return jnp.swapaxes(array, 0, 1).reshape(plan.total, -1)

    att_low = by_member(attended.astype(bf16))
    second = resid + plan.sum_tokens(
        lambda lo, hi: jnp.einsum("th,dh->td", att_low[lo:hi], w_output, preferred_element_type=f32)
    )
    h_second, n_second, i_second = layer_norm(second, gains[2], gains[3])
    a_second = plan.gather_tokens(h_second.astype(bf16))
    gated = jnp.einsum("td,df->tf", a_second, w_gate, preferred_element_type=f32)
    gate = gated[:, :hidden]
    upper = gated[:, hidden:]
    sigma = jax.nn.sigmoid(gate)
    active_gate = gate * sigma
    hid = (active_gate * upper).astype(bf16)
    result = second + plan.sum_tokens(
        lambda lo, hi: jnp.einsum("tf,df->td", hid[lo:hi], w_down, preferred_element_type=f32)
    )
    layer_out = plan.outputs_of_rows(result.astype(bf16), quarter)

    real = (own_position[None, :] < lens[:, None]).reshape(share, 1)
    grad_y = jnp.where(real, plan.inputs_of_rows(cotangent).astype(f32), 0.0)
    grad_y_all = plan.gather_tokens(grad_y.astype(bf16))
    grad_hidden = jnp.einsum(
        "td,df->tf", grad_y_all, w_down, preferred_element_type=f32
    ).astype(bf16)
    grad_gate_val = grad_hidden * upper * (sigma * (1.0 + gate * (1.0 - sigma)))
    grad_up_val = grad_hidden * active_gate
    grad_gated = jnp.concatenate([grad_gate_val, grad_up_val], 1).astype(bf16)
    grad_down = plan.collect_grad(grad_y_all, hid)
    grad_h2 = plan.sum_tokens(
        lambda lo, hi: jnp.einsum("tf,df->td", grad_gated[lo:hi], w_gate, preferred_element_type=f32)
    )
    grad_gate = plan.collect_grad(a_second, grad_gated)
    grad_second = grad_y + norm_back(grad_h2, n_second, i_second, gains[2])
    grad_second_all = plan.gather_tokens(grad_second.astype(bf16))
    grad_att = jnp.einsum(
        "td,dh->th", grad_second_all, w_output, preferred_element_type=f32
    ).astype(bf16)
    grad_output = plan.collect_grad(grad_second_all, att_low)
    grad_att = jnp.swapaxes(
        grad_att.reshape(plan.members, rows, groups * quarter, heads_here, HD), 0, 1
    ).reshape(rows, length, heads_here, HD)
    delta = jnp.transpose(jnp.sum(grad_att.astype(f32) * attended, -1), (0, 2, 1))
    grad_val = jnp.einsum(
        "rhqk,rqhd->rkhd", probs.astype(bf16), grad_att, preferred_element_type=f32
    )
    grad_prob = jnp.einsum("rqhd,rkhd->rhqk", grad_att, vals, preferred_element_type=f32)
    grad_score = (probs * (grad_prob - delta[..., None])).astype(bf16)
    grad_query = jnp.einsum("rhqk,rkhd->rqhd", grad_score, keys, preferred_element_type=f32)
    grad_key = jnp.einsum("rhqk,rqhd->rkhd", grad_score, query, preferred_element_type=f32)
    grad_q_raw = rotate(grad_query * 0.125, cosine, -sine)
    grad_k_raw = rotate(grad_key, cosine, -sine)
    grad_mixed = by_member(jnp.stack([grad_q_raw, grad_k_raw, grad_val], 2).astype(bf16))
    grad_h1 = plan.sum_tokens(
        lambda lo, hi: jnp.einsum("tf,df->td", grad_mixed[lo:hi], w_entry, preferred_element_type=f32)
    )
    grad_entry = plan.collect_grad(a_first, grad_mixed)
    grad_input = grad_second + norm_back(grad_h1, n_first, i_first, gains[0])
    input_grad = plan.outputs_of_rows(grad_input.astype(bf16), quarter)

    sums = jnp.stack(
        [
            jnp.sum(grad_h1 * n_first, 0),
            jnp.sum(grad_h1, 0),
            jnp.sum(grad_h2 * n_second, 0),
            jnp.sum(grad_h2, 0),
        ]
    )
    bias_sum = jnp.sum(grad_mixed.astype(f32), 0)
    for mask in plan.outer:
        bias_sum = bias_sum + swap(bias_sum, "seq", mask)
    bias_sum = bias_sum.reshape(3, heads_here, HD)
    got = [bias_sum] + [swap(bias_sum, "seq", plan.inner_mask(j)) for j in range(1, parts)]
    bias_sum = joined(pick(got, plan.part_flags), 1)
    slim = entry_bias.shape[2]
    grad_bias = lax.dynamic_slice_in_dim(bias_sum, plan.seq * slim, slim, 2)
    set_width = width // groups
    pieces = {j: sums[:, j * set_width : (j + 1) * set_width] for j in range(groups)}
    for axis, mask, bit in plan.group_steps:
        keys_sent = sorted(k for k in pieces if k & bit)
        got = swap(jnp.stack([pieces[k] for k in keys_sent]), axis, mask)
        pieces = {
            **{k: v for k, v in pieces.items() if not k & bit and k | bit not in keys_sent},
            **{k ^ bit: pieces[k ^ bit] + got[i] for i, k in enumerate(keys_sent)},
        }
    slim = set_width // parts
    mine = pick([pieces[0][:, h * slim : (h + 1) * slim] for h in range(parts)], plan.part_flags)
    grad_norm = mine[0]
    for j in range(1, parts):
        grad_norm = grad_norm + swap(mine[j], "seq", plan.inner_mask(j))
    for mask in plan.tp_masks:
        grad_norm = grad_norm + swap(grad_norm, "tp", mask)

    def whole(blocks, shape):
        middle = shape[1:-1]
        return jnp.concatenate([b.reshape((b.shape[0],) + middle + (-1,)) for b in blocks], -1)

    reduced = (
        grad_norm,
        whole(grad_entry, entry_weight.shape),
        grad_bias,
        whole(grad_output, output_weight.shape),
        whole(grad_gate, gate_weight.shape),
        whole(grad_down, down_weight.shape),
    )
    masters = (norm_params, entry_weight, entry_bias, output_weight, gate_weight, down_weight)
    moments = (moment_norm, moment_entry, moment_bias, moment_output, moment_gate, moment_down)
    averages = (
        average_norm,
        average_entry,
        average_bias,
        average_output,
        average_gate,
        average_down,
    )
    beta = min(0.999, (1 + STEP) / (10 + STEP))
    news, new_weights, smooths, copies = ([], [], [], [])
    for index in range(6):
        grad = reduced[index] + decays[index] * masters[index]
        moment = 0.9 * moments[index] + grad
        weight = masters[index] - rates[index] * (grad + 0.9 * moment)
        news.append(moment)
        new_weights.append(weight)
        smooths.append(beta * averages[index] + (1.0 - beta) * weight)
        copies.append(weight.astype(bf16))
    return (layer_out, input_grad, *news, *new_weights, *smooths, *copies)


def solution(mesh):
    in_specs = (
        P("seq", None, None),
        P("seq", None, None),
        P(),
        P(None, "seq"),
        P("seq", None, "tp"),
        P(None, "tp", "seq"),
        P("seq", "tp"),
        P("seq", None, "tp"),
        P("seq", "tp"),
        P(None, "seq"),
        P("seq", None, "tp"),
        P(None, "tp", "seq"),
        P("seq", "tp"),
        P("seq", None, "tp"),
        P("seq", "tp"),
        P(None, "seq"),
        P("seq", None, "tp"),
        P(None, "tp", "seq"),
        P("seq", "tp"),
        P("seq", None, "tp"),
        P("seq", "tp"),
    )
    out_specs = (
        P("seq", None, None),
        P("seq", None, None),
        P(None, "seq"),
        P("seq", None, "tp"),
        P(None, "tp", "seq"),
        P("seq", "tp"),
        P("seq", None, "tp"),
        P("seq", "tp"),
        P(None, "seq"),
        P("seq", None, "tp"),
        P(None, "tp", "seq"),
        P("seq", "tp"),
        P("seq", None, "tp"),
        P("seq", "tp"),
        P(None, "seq"),
        P("seq", None, "tp"),
        P(None, "tp", "seq"),
        P("seq", "tp"),
        P("seq", None, "tp"),
        P("seq", "tp"),
        P(None, "seq"),
        P("seq", None, "tp"),
        P(None, "tp", "seq"),
        P("seq", "tp"),
        P("seq", None, "tp"),
        P("seq", "tp"),
    )
    return jax.shard_map(body, mesh=mesh, in_specs=in_specs, out_specs=out_specs, check_vma=False)
```

```python
import numpy as np

import jax
import jax.numpy as jnp
from jax import lax
from jax.experimental import pallas as pl
from jax.experimental.layout import Layout, with_layout_constraint
from jax.experimental.pallas import tpu as pltpu
from jax.sharding import PartitionSpec as P

HD = 64
ROT = 16
STEP = 10

eps = 1e-05
rates = (0.0005, 0.0002, 0.0025, 0.004, 0.0002, 6e-05)
decays = (0.0, 0.0001, 0.0, 0.0001, 0.0001, 0.0001)
bf16 = jnp.bfloat16
f32 = jnp.float32


def swap(array, axis, mask):
    pairs = [(i, i ^ mask) for i in range(lax.axis_size(axis))]
    return lax.ppermute(array, axis, pairs)


def pick(parts, flags):
    count = len(parts)
    for place, flag in enumerate(flags):
        bit = count >> (place + 1)
        parts = [jnp.where(flag, parts[j ^ bit], parts[j]) for j in range(count)]
    return parts


def joined(parts, axis=0):
    return parts[0] if len(parts) == 1 else jnp.concatenate(parts, axis)


def gather(piece, steps):
    pieces = {0: piece}
    rows = piece.shape[0]
    for axis, mask, bit in steps:
        keys = sorted(pieces)
        got = swap(joined([pieces[k] for k in keys]), axis, mask)
        for place, k in enumerate(keys):
            pieces[k | bit] = got[place * rows : (place + 1) * rows]
    return pieces


def scatter(pieces, steps):
    for axis, mask, bit in steps:
        keys = sorted(k for k in pieces if k & bit)
        got = swap(joined([pieces[k].astype(bf16) for k in keys]), axis, mask)
        rows = got.shape[0] // len(keys)
        kept = {k: v for k, v in pieces.items() if not k & bit}
        for place, k in enumerate(keys):
            kept[k ^ bit] = kept[k ^ bit].astype(f32) + got[place * rows : (place + 1) * rows].astype(f32)
        pieces = kept
    return pieces[0]


class Plan:
    def __init__(self, rows):
        self.n_seq = lax.axis_size("seq")
        self.n_tp = lax.axis_size("tp")
        self.seq = lax.axis_index("seq")
        self.tp = lax.axis_index("tp")
        bits = self.n_seq.bit_length() - 1
        self.inner = [1 << i for i in range(bits // 2)][::-1]
        self.outer = [1 << i for i in range(bits) if (1 << i) not in self.inner][::-1]
        self.groups = 1 << len(self.outer)
        self.parts = 1 << len(self.inner)
        self.rows = rows // self.groups
        self.group_flags = [(self.seq & m) != 0 for m in self.outer]
        self.part_flags = [(self.seq & m) != 0 for m in self.inner]
        self.tp_masks = [1 << i for i in range(self.n_tp.bit_length() - 1)]
        self.tp_flags = [(self.tp & m) != 0 for m in self.tp_masks[::-1]]
        self.group = self.index(self.group_flags)
        order = [("tp", m) for m in self.tp_masks] + [("seq", m) for m in self.inner]
        self.members = 1 << len(order)
        self.steps = [(axis, mask, self.members >> (i + 1)) for i, (axis, mask) in enumerate(order)]
        self.group_steps = [("seq", m, self.groups >> (i + 1)) for i, m in enumerate(self.outer)]

    def index(self, flags):
        value = jnp.int32(0)
        for flag in flags:
            value = value * 2 + flag.astype(jnp.int32)
        return value

    def outer_mask(self, j):
        return sum(m for i, m in enumerate(self.outer) if j & (self.groups >> (i + 1)))

    def inner_mask(self, j):
        return sum(m for i, m in enumerate(self.inner) if j & (self.parts >> (i + 1)))

    def member_masks(self, k):
        seq = sum(m for a, m, bit in self.steps if a == "seq" and k & bit)
        tp = sum(m for a, m, bit in self.steps if a == "tp" and k & bit)
        return seq, tp

    def arranged(self, array):
        wide = array.shape[-1] // self.n_seq
        places = [self.outer_mask(g) | self.inner_mask(h) for g in range(self.groups) for h in range(self.parts)]
        return joined([array[..., p * wide : (p + 1) * wide] for p in places], -1)

    def restored(self, array):
        wide = array.shape[-1] // self.n_seq
        blocks = [None] * self.n_seq
        for g in range(self.groups):
            for h in range(self.parts):
                at = g * self.parts + h
                blocks[self.outer_mask(g) | self.inner_mask(h)] = array[..., at * wide : (at + 1) * wide]
        return joined(blocks, -1)

    def lists(self):
        return [
            [self.outer_mask(g) | self.inner_mask(h) for g in range(self.groups)] for h in range(self.parts)
        ]

    def chosen(self, j, part, all_rows):
        row = lax.broadcasted_iota(jnp.int32, (self.rows * part, part * all_rows), 0)
        column = lax.broadcasted_iota(jnp.int32, (self.rows * part, part * all_rows), 1)
        source = (row % part) * all_rows + (self.group ^ j) * self.rows + row // part
        return (column == source).astype(bf16)

    def outgoing_rows(self, array):
        block, all_rows, width = array.shape
        part = block // self.n_tp
        size = part * all_rows
        own = lax.dynamic_slice_in_dim(array.reshape(-1, width), self.tp * size, size, 0)
        return [
            jnp.dot(self.chosen(j, part, all_rows), own, preferred_element_type=f32).astype(bf16)
            for j in range(self.groups)
        ]

    def over_groups(self, pieces):
        return [swap(piece, "seq", self.outer_mask(j)) if j else piece for j, piece in enumerate(pieces)]

    def returning_rows(self, tokens):
        table = self.restored(tokens)
        size = table.shape[0] // self.groups
        return [table[j * size : (j + 1) * size] for j in range(self.groups)]

    def returned_rows(self, got, part, all_rows):
        back = jnp.concatenate([self.chosen(j, part, all_rows) for j in range(self.groups)], 0)
        return jnp.einsum("sp,sd->pd", back, jnp.concatenate(got, 0), preferred_element_type=f32).astype(bf16)

    def of_tp(self, pieces):
        return joined(pick([pieces[k] for k in range(self.n_tp)], self.tp_flags), 0)

    def chips_sides(self, piece):
        far = self.steps[1:]
        if len(far) != 2:
            return gather(piece, far)
        return [swap(piece, axis, mask) for axis, mask, _ in far]

    def chips_corner(self, piece, sides):
        far = self.steps[1:]
        if len(far) != 2:
            return sides
        half = piece.shape[0] // 2
        (axis_x, mask_x, _), (axis_z, mask_z, _) = far
        return [swap(sides[0][:half], axis_z, mask_z), swap(sides[1][half:], axis_x, mask_x)]

    def chips_near(self, piece, sides, corner):
        if len(self.steps) != 3:
            return joined([sides[k] for k in sorted(sides)])
        return jnp.concatenate([piece, sides[1], sides[0], corner[0], corner[1]], 0)

    def swap_core(self, array):
        axis, mask, _ = self.steps[0]
        return swap(array, axis, mask)

    def sum_corner(self, near):
        far = self.steps[1:]
        if len(far) != 2:
            chips = 1 << len(far)
            rows = near.shape[0] // chips
            return [scatter({k: near[k * rows : (k + 1) * rows] for k in range(chips)}, far)]
        (axis_x, mask_x, _), (axis_z, mask_z, _) = far
        rows = near.shape[0] // 4
        half = rows // 2
        corner = near[3 * rows :].astype(bf16)
        return [swap(corner[:half], axis_x, mask_x), swap(corner[half:], axis_z, mask_z)]

    def sum_sides(self, near, corner):
        far = self.steps[1:]
        if len(far) != 2:
            return corner
        (axis_x, mask_x, _), (axis_z, mask_z, _) = far
        rows = near.shape[0] // 4
        half = rows // 2
        one, two = near[rows : 2 * rows], near[2 * rows : 3 * rows]
        for_z = jnp.concatenate([one[:half] + corner[0].astype(f32), one[half:]], 0).astype(bf16)
        for_x = jnp.concatenate([two[:half], two[half:] + corner[1].astype(f32)], 0).astype(bf16)
        return [swap(for_z, axis_z, mask_z), swap(for_x, axis_x, mask_x)]

    def sum_end(self, near, sides):
        if len(self.steps) != 3:
            return sides[0]
        rows = near.shape[0] // 4
        return near[:rows] + sides[0].astype(f32) + sides[1].astype(f32)

    def spread_mine(self, mine, axis):
        got = [mine[0]] + [swap(mine[j], "seq", self.inner_mask(j)) for j in range(1, self.parts)]
        return joined(pick(got, self.part_flags), axis)

    def collect_home(self, block_sum):
        rows = block_sum.shape[0] // self.parts
        blocks = [block_sum[h * rows : (h + 1) * rows] for h in range(self.parts)]
        mine = pick(blocks, self.part_flags)
        got = [mine[0].astype(f32)] + [
            swap(mine[j].astype(bf16), "seq", self.inner_mask(j)).astype(f32) for j in range(1, self.parts)
        ]
        return pick(got, self.part_flags)

    def all_blocks(self, block):
        return lax.all_gather(block, "seq", axis_index_groups=self.lists(), axis=0, tiled=True)

    def sum_blocks(self, product):
        return lax.psum_scatter(
            product, "seq", scatter_dimension=0, axis_index_groups=self.lists(), tiled=True
        )


def hold(*values):
    return lax.optimization_barrier(values)


def layer_norm(values, gain, shift):
    center = values - jnp.mean(values, -1, keepdims=True)
    var = jnp.mean(center * center, -1, keepdims=True)
    inverse = lax.rsqrt(var + eps)
    normed = center * inverse
    return (normed * gain + shift, normed, inverse)


def norm_back(grad, normed, inverse, gain):
    scaled = grad * gain
    inner = (
        scaled
        - jnp.mean(scaled, -1, keepdims=True)
        - normed * jnp.mean(scaled * normed, -1, keepdims=True)
    )
    return inner * inverse


def turning(position):
    lane = jnp.arange(128, dtype=jnp.int32) % HD
    half = ROT // 2
    freq = 10000.0 ** (-(lane % half).astype(f32) / half)
    angle = position.astype(f32)[:, None] * jnp.where(lane < ROT, freq, 0.0)[None, :]
    return jnp.cos(angle), jnp.sin(angle) * jnp.where(lane < half, -1.0, 1.0)[None, :]


def turned(values, cosine, sine):
    wide = values.shape[1]
    half = ROT // 2
    lane = lax.broadcasted_iota(jnp.int32, values.shape, 1) & (HD - 1)
    partner = jnp.where(lane < half, pltpu.roll(values, wide - half, 1), pltpu.roll(values, half, 1))
    return values * cosine + partner * sine


def widened(table, wide):
    return table if wide == table.shape[1] else jnp.concatenate([table] * (wide // table.shape[1]), 1)


def head_lanes(shape, head):
    return lax.broadcasted_iota(jnp.int32, shape, len(shape) - 1) // HD == head


def dot(left, right, over):
    return lax.dot_general(left, right, (over, ((), ())), preferred_element_type=f32)


def forward_kernel(lens, mixed, shift, cosine, sine, column, line, qkv_ref, low_ref, full_ref, sums_ref):
    wide = mixed.shape[-1] // 3
    length = line.shape[1]
    values = mixed[...].reshape(length, 3 * wide) + shift[...]
    cos, sin = widened(cosine[...], wide), widened(sine[...], wide)
    query = (turned(values[:, :wide], cos, sin) * 0.125).astype(bf16)
    keys = turned(values[:, wide : 2 * wide], cos, sin).astype(bf16)
    vals = values[:, 2 * wide :].astype(bf16)
    for place, part in enumerate((query, keys, vals)):
        qkv_ref[:, :, :, place * wide : (place + 1) * wide] = part.reshape(qkv_ref.shape[:-1] + (wide,))
    size = min(512, length)
    blocks = mixed.shape[0] * size // length
    limit = lens[pl.program_id(0)]
    for start in range(0, length, size):
        rows = slice(start, start + size)
        valid = (line[...] <= column[rows]) & (line[...] < limit)
        out = jnp.zeros((size, wide), f32)
        kept = jnp.zeros((size, 128), f32)
        for head in range(wide // HD):
            here = head_lanes((size, wide), head)
            scores = dot(jnp.where(here, query[rows], 0), keys, ((1,), (1,)))
            scores = jnp.where(valid, scores, -1e30)
            top = jnp.max(scores, 1, keepdims=True)
            weights = jnp.exp(scores - top)
            total = jnp.sum(weights, 1, keepdims=True)
            probs = (weights * (1.0 / total)).astype(bf16)
            out = jnp.where(here, dot(probs, vals, ((1,), (0,))), out)
            lane = lax.broadcasted_iota(jnp.int32, kept.shape, 1)
            kept = jnp.where(lane == head, top + jnp.log(total), kept)
        at = slice(start // size * blocks, (start // size + 1) * blocks)
        low_ref[at] = out.astype(bf16).reshape((blocks,) + low_ref.shape[1:])
        full_ref[at] = out.reshape((blocks,) + full_ref.shape[1:])
        sums_ref[0, rows] = kept


def backward_kernel(lens, qkv, grad, full, sums, cosine, sine, column, line, out_ref, bias_ref):
    wide = grad.shape[-1]
    length = line.shape[1]
    values = qkv[...].reshape(length, 3 * wide)
    query, keys, vals = (values[:, i * wide : (i + 1) * wide] for i in range(3))
    grads = grad[...].reshape(length, wide)
    attended = full[...].reshape(length, wide)
    size = min(512, length)
    limit = lens[pl.program_id(0)]
    grad_query = []
    grad_key = jnp.zeros((length, wide), f32)
    grad_val = jnp.zeros((length, wide), f32)
    for start in range(0, length, size):
        rows = slice(start, start + size)
        valid = (line[...] <= column[rows]) & (line[...] < limit)
        both = grads[rows].astype(f32) * attended[rows]
        grad_here = jnp.zeros((size, wide), f32)
        for head in range(wide // HD):
            here = head_lanes((size, wide), head)
            own_query = jnp.where(here, query[rows], 0)
            own_grad = jnp.where(here, grads[rows], 0)
            own_keys = jnp.where(head_lanes((length, wide), head), keys, 0)
            delta = jnp.sum(jnp.where(here, both, 0.0), 1, keepdims=True)
            scores = dot(own_query, keys, ((1,), (1,)))
            probs = jnp.where(valid, jnp.exp(scores - sums[0, rows, head : head + 1]), 0.0)
            grad_val = grad_val + dot(probs.astype(bf16), own_grad, ((0,), (0,)))
            grad_prob = dot(own_grad, vals, ((1,), (1,)))
            grad_score = (probs * (grad_prob - delta)).astype(bf16)
            grad_here = grad_here + dot(grad_score, own_keys, ((1,), (0,)))
            grad_key = grad_key + dot(grad_score, own_query, ((0,), (0,)))
        grad_query.append(grad_here)
    cos, sin = widened(cosine[...], wide), -widened(sine[...], wide)
    grad_query = turned(joined(grad_query) * 0.125, cos, sin)
    grad_key = turned(grad_key, cos, sin)
    for place, part in enumerate((grad_query, grad_key, grad_val)):
        part = part.astype(bf16)
        at = slice(place * wide, (place + 1) * wide)
        out_ref[:, :, :, at] = part.reshape(out_ref.shape[:-1] + (wide,))
        bias_ref[0, :, at] = jnp.broadcast_to(jnp.sum(part.astype(f32), 0, keepdims=True), (8, wide))


def of_row(array):
    blocks, _, places, wide = array.shape
    return pl.BlockSpec((blocks, 1, places, wide), lambda r, lens: (0, r, 0, 0))


def entire(array):
    return pl.BlockSpec(array.shape, lambda r, lens: (0,) * array.ndim)


def attend_forward(mixed, shift, tables, lens):
    blocks, rows, places, wide = mixed.shape
    wide = wide // 3
    length = blocks * places
    out = [
        jax.ShapeDtypeStruct((blocks, rows, places, 3 * wide), bf16),
        jax.ShapeDtypeStruct((blocks, rows, places, wide), bf16),
        jax.ShapeDtypeStruct((blocks, rows, places, wide), f32),
        jax.ShapeDtypeStruct((rows, length, 128), f32),
    ]
    return pl.pallas_call(
        forward_kernel,
        out_shape=out,
        grid_spec=pltpu.PrefetchScalarGridSpec(
            num_scalar_prefetch=1,
            grid=(rows,),
            in_specs=[of_row(mixed), entire(shift)] + [entire(t) for t in tables],
            out_specs=[of_row(o) for o in out[:3]]
            + [pl.BlockSpec((1, length, 128), lambda r, lens: (r, 0, 0))],
        ),
        compiler_params=pltpu.CompilerParams(vmem_limit_bytes=40 << 20),
        name="attend_forward",
    )(lens, mixed, shift, *tables)


def attend_backward(qkv, grad, full, sums, tables, lens):
    blocks, rows, places, wide = grad.shape
    length = blocks * places
    out = [
        jax.ShapeDtypeStruct(qkv.shape, bf16),
        jax.ShapeDtypeStruct((rows, 8, 3 * wide), f32),
    ]
    return pl.pallas_call(
        backward_kernel,
        out_shape=out,
        grid_spec=pltpu.PrefetchScalarGridSpec(
            num_scalar_prefetch=1,
            grid=(rows,),
            in_specs=[
                of_row(qkv),
                of_row(grad),
                of_row(full),
                pl.BlockSpec((1, length, 128), lambda r, lens: (r, 0, 0)),
            ]
            + [entire(t) for t in tables],
            out_specs=[of_row(out[0]), pl.BlockSpec((1, 8, 3 * wide), lambda r, lens: (r, 0, 0))],
        ),
        compiler_params=pltpu.CompilerParams(vmem_limit_bytes=48 << 20),
        name="attend_backward",
    )(lens, qkv, grad, full, sums, *tables)


def body(
    inputs,
    cotangent,
    lengths,
    norm_params,
    entry_weight,
    entry_bias,
    output_weight,
    gate_weight,
    down_weight,
    moment_norm,
    moment_entry,
    moment_bias,
    moment_output,
    moment_gate,
    moment_down,
    average_norm,
    average_entry,
    average_bias,
    average_output,
    average_gate,
    average_down,
):
    plan = Plan(inputs.shape[1])
    groups, parts, rows = plan.groups, plan.parts, plan.rows
    block_len, _, width = inputs.shape
    tp_width = entry_weight.shape[2]
    head_width = tp_width // parts
    heads_here = head_width // HD
    hidden = gate_weight.shape[2] // parts
    quarter = block_len // plan.n_tp
    share = rows * groups * quarter
    plan.total = share * plan.members
    length = block_len * plan.n_seq

    member_seq = np.array([plan.member_masks(k)[0] for k in range(plan.members)], np.int32)
    member_tp = np.array([plan.member_masks(k)[1] for k in range(plan.members)], np.int32)
    sender = np.array([plan.outer_mask(j) for j in range(groups)], np.int32)
    seq_at = plan.seq ^ (member_seq[:, None] | sender[None, :])
    tp_at = plan.tp ^ member_tp
    position = (
        (seq_at * block_len)[:, :, None]
        + (tp_at * quarter)[:, None, None]
        + np.arange(quarter, dtype=np.int32)[None, None, :]
    )
    lens = lax.dynamic_slice_in_dim(lengths, plan.group * rows, rows, 0)

    def over_masks(array, masks):
        sums = [0]
        for mask in masks:
            sums = sums + [m | mask for m in sums]
        return [swap(array, "seq", m) for m in sums[1:]]

    def total_of(array, got):
        for other in got:
            array = array + other
        return array

    lane_block = lax.broadcasted_iota(jnp.int32, (4, width), 1) // norm_params.shape[1]
    small = jnp.where(lane_block == plan.seq, jnp.tile(norm_params.astype(bf16), (1, plan.n_seq)), 0)
    slim = entry_bias.shape[2]
    slot = lax.broadcasted_iota(jnp.int32, (slim, HD), 1) == plan.seq * slim + lax.broadcasted_iota(
        jnp.int32, (slim, HD), 0
    )
    placed = jnp.dot(entry_bias.reshape(-1, slim).astype(bf16), slot.astype(bf16), preferred_element_type=f32)
    placed = placed.astype(bf16).reshape(1, 3 * tp_width)
    placed = jnp.pad(placed, ((0, 0), (0, width - 3 * tp_width)))
    small = jnp.concatenate([small, placed], 0)
    seq_masks = [1 << i for i in range(plan.n_seq.bit_length() - 1)]
    last_mask = plan.outer[-1]
    first_masks = [m for m in seq_masks if m != last_mask]

    def columns(array, h, size):
        return array[..., h * size : (h + 1) * size].astype(bf16).reshape(array.shape[0], -1)

    def turned_columns(array, h):
        return array[:, h * hidden : (h + 1) * hidden].astype(bf16).T

    small_got = over_masks(small, first_masks)
    outgoing = plan.outgoing_rows(inputs)
    resid = plan.over_groups(outgoing)
    attn_mine = pick(
        [
            jnp.concatenate(
                [columns(entry_weight, h, head_width), columns(output_weight, h, head_width)], 1
            )
            for h in range(parts)
        ],
        plan.part_flags,
    )
    attn_block = plan.spread_mine(attn_mine, 0)
    gate_mine = pick([columns(gate_weight, h, hidden) for h in range(parts)], plan.part_flags)
    small, small_got, resid, attn_block, cotangent, gate_mine, position, down_weight = hold(
        small, small_got, resid, attn_block, cotangent, gate_mine, position, down_weight
    )

    w_attn = plan.all_blocks(attn_block)
    small = total_of(small, small_got)
    small_got = over_masks(small, [last_mask])
    gate_block = plan.spread_mine(gate_mine, 0)
    outgoing = plan.outgoing_rows(cotangent)
    small, small_got, resid, gate_block, outgoing, position, down_weight = hold(
        small, small_got, resid, gate_block, outgoing, position, down_weight
    )

    small = total_of(small, small_got)
    gains = plan.arranged(small[:4]).astype(f32)
    resid = plan.arranged(jnp.concatenate(resid, 0)).astype(f32)
    h_first, n_first, i_first = layer_norm(resid, gains[0], gains[1])
    low_first = h_first.astype(bf16)
    sides = plan.chips_sides(low_first)
    row_position = position.reshape(length)
    tables = turning(row_position) + (row_position[:, None], row_position[None, :])
    down_mine = pick([columns(down_weight, h, hidden) for h in range(parts)], plan.part_flags)
    low_first, sides, tables, down_mine, outgoing, gate_block = hold(
        low_first, sides, tables, down_mine, outgoing, gate_block
    )

    corner = plan.chips_corner(low_first, sides)
    down_block = plan.spread_mine(down_mine, 0)
    low_first, sides, corner, down_block, outgoing = hold(low_first, sides, corner, down_block, outgoing)
    near = plan.chips_near(low_first, sides, corner)
    other = plan.swap_core(near)
    grad_y = plan.over_groups(outgoing)
    near, other, grad_y, w_attn, gate_block, down_block = hold(
        near, other, grad_y, w_attn, gate_block, down_block
    )
    a_first = jnp.concatenate([near, other], 0)
    w_gate = plan.all_blocks(gate_block)
    own_position = jnp.broadcast_to(position[0][:, None, :], (groups, rows, quarter))
    real = (own_position < lens[None, :, None]).reshape(share, 1)
    grad_y = plan.arranged(jnp.concatenate(grad_y, 0))
    grad_y = jnp.where(real, grad_y, 0)
    y_sides = plan.chips_sides(grad_y)

    w_entry = w_attn[:, : 3 * head_width]
    w_output = w_attn[:, 3 * head_width :]
    mixed = jnp.einsum("td,df->tf", a_first, w_entry, preferred_element_type=f32)
    mixed = mixed.reshape(plan.members * groups, rows, quarter, 3 * head_width)
    biases = [
        jnp.concatenate(
            [
                small[4:, c * tp_width + h * head_width : c * tp_width + (h + 1) * head_width]
                for c in range(3)
            ],
            1,
        )
        for h in range(parts)
    ]
    entry_shift = pick(biases, plan.part_flags)[0].astype(f32)
    qkv, att_low, attended, score_sums = attend_forward(mixed, entry_shift, tables, lens)
    att_low = att_low.reshape(plan.total, head_width)

    def output_product(lo, hi):
        return jnp.einsum("th,dh->td", att_low[lo:hi], w_output, preferred_element_type=f32)

    half = plan.total // 2
    far_product = output_product(half, plan.total).astype(bf16)
    far_product, grad_y, y_sides, down_block = hold(far_product, grad_y, y_sides, down_block)

    got = plan.swap_core(far_product)
    product = output_product(0, half)
    y_corner = plan.chips_corner(grad_y, y_sides)
    product, got, y_corner = hold(product, got, y_corner)

    near = product + got.astype(f32)
    corner = plan.sum_corner(near)
    y_near = plan.chips_near(grad_y, y_sides, y_corner)
    near, corner, y_near = hold(near, corner, y_near)
    sides = plan.sum_sides(near, corner)
    y_other = plan.swap_core(y_near)
    near, sides, y_near, y_other, down_block = hold(near, sides, y_near, y_other, down_block)

    second = resid + plan.sum_end(near, sides)
    h_second, n_second, i_second = layer_norm(second, gains[2], gains[3])
    low_second = h_second.astype(bf16)
    sides = plan.chips_sides(low_second)
    grad_y_all = jnp.concatenate([y_near, y_other], 0)
    second, low_second, sides, grad_y_all = hold(second, low_second, sides, grad_y_all)
    corner = plan.chips_corner(low_second, sides)
    low_second, sides, corner, w_gate, down_block = hold(low_second, sides, corner, w_gate, down_block)
    w_down = plan.all_blocks(down_block)
    near = plan.chips_near(low_second, sides, corner)
    other = plan.swap_core(near)
    near, other = hold(near, other)

    a_second = jnp.concatenate([near, other], 0)
    gated = jnp.einsum("td,df->tf", a_second, w_gate, preferred_element_type=f32)
    gate = gated[:, :hidden]
    upper = gated[:, hidden:]
    sigma = jax.nn.sigmoid(gate)
    active_gate = gate * sigma
    hid = (active_gate * upper).astype(bf16)
    grad_down = jnp.einsum("td,tf->df", grad_y_all, hid, preferred_element_type=f32).astype(bf16)
    hid, grad_down, w_down = hold(hid, grad_down, w_down)
    down_sum = plan.sum_blocks(grad_down)
    grad_hidden = jnp.einsum(
        "td,df->tf", grad_y_all, w_down, preferred_element_type=f32
    ).astype(bf16)
    grad_gate_val = grad_hidden * upper * (sigma * (1.0 + gate * (1.0 - sigma)))
    grad_up_val = grad_hidden * active_gate
    grad_gated = jnp.concatenate([grad_gate_val, grad_up_val], 1).astype(bf16)

    def gate_product(lo, hi):
        return jnp.einsum("tf,df->td", grad_gated[lo:hi], w_gate, preferred_element_type=f32)

    def down_product(lo, hi):
        return jnp.einsum("tf,df->td", hid[lo:hi], w_down, preferred_element_type=f32)

    far_product = gate_product(half, plan.total).astype(bf16)
    hid, grad_gated, far_product = hold(hid, grad_gated, far_product)

    got = plan.swap_core(far_product)
    product = gate_product(0, half)
    product, got, a_second, hid, grad_gated = hold(product, got, a_second, hid, grad_gated)

    near = product + got.astype(f32)
    corner = plan.sum_corner(near)
    grad_gate = jnp.einsum("td,tf->df", a_second, grad_gated, preferred_element_type=f32).astype(bf16)
    near, corner, grad_gate, hid, down_sum = hold(near, corner, grad_gate, hid, down_sum)
    gate_sum = plan.sum_blocks(grad_gate)
    sides = plan.sum_sides(near, corner)
    out_far = down_product(half, plan.total).astype(bf16)
    near, sides, out_far, hid, down_sum = hold(near, sides, out_far, hid, down_sum)

    out_got = plan.swap_core(out_far)
    grad_h2 = plan.sum_end(near, sides)
    grad_second = grad_y.astype(f32) + norm_back(grad_h2, n_second, i_second, gains[2])
    low_grad = grad_second.astype(bf16)
    sides = plan.chips_sides(low_grad)
    out_near = down_product(0, half)
    low_grad, sides, out_near, out_got, grad_h2, grad_second = hold(
        low_grad, sides, out_near, out_got, grad_h2, grad_second
    )
    out_near = out_near + out_got.astype(f32)
    corner = plan.chips_corner(low_grad, sides)
    out_corner = plan.sum_corner(out_near)
    low_grad, sides, corner, out_corner, out_near = hold(low_grad, sides, corner, out_corner, out_near)

    near = plan.chips_near(low_grad, sides, corner)
    other = plan.swap_core(near)
    near, other = hold(near, other)
    grad_second_all = jnp.concatenate([near, other], 0)
    grad_att = jnp.einsum(
        "td,dh->th", grad_second_all, w_output, preferred_element_type=f32
    ).astype(bf16)
    grad_att = grad_att.reshape(attended.shape)
    grad_mixed, bias_sum = attend_backward(qkv, grad_att, attended, score_sums, tables, lens)
    grad_mixed = grad_mixed.reshape(plan.total, 3 * head_width)

    def entry_product(lo, hi):
        return jnp.einsum("tf,df->td", grad_mixed[lo:hi], w_entry, preferred_element_type=f32)

    far_product = entry_product(half, plan.total).astype(bf16)
    out_sides = plan.sum_sides(out_near, out_corner)
    far_product, grad_mixed, bias_sum, out_sides, out_near = hold(
        far_product, grad_mixed, bias_sum, out_sides, out_near
    )

    got = plan.swap_core(far_product)
    product = entry_product(0, half)
    grad_attn = jnp.concatenate(
        [
            jnp.einsum("td,tf->df", a_first, grad_mixed, preferred_element_type=f32).astype(bf16),
            jnp.einsum("td,tf->df", grad_second_all, att_low, preferred_element_type=f32).astype(bf16),
        ],
        1,
    )
    product, got, grad_attn, bias_sum, down_sum = hold(product, got, grad_attn, bias_sum, down_sum)

    near = product + got.astype(f32)
    corner = plan.sum_corner(near)
    near, corner, bias_sum, down_sum, grad_attn = hold(near, corner, bias_sum, down_sum, grad_attn)
    sides = plan.sum_sides(near, corner)
    result = second + plan.sum_end(out_near, out_sides)
    out_returning = plan.returning_rows(result.astype(bf16))
    near, sides, out_returning, bias_sum, down_sum, gate_sum, grad_attn = hold(
        near, sides, out_returning, bias_sum, down_sum, gate_sum, grad_attn
    )
    attn_sum = plan.sum_blocks(grad_attn)

    grad_h1 = plan.sum_end(near, sides)
    grad_input = grad_second + norm_back(grad_h1, n_first, i_first, gains[0])
    back = plan.over_groups(plan.returning_rows(grad_input.astype(bf16)))
    out_back = plan.over_groups(out_returning)
    gate_home = plan.collect_home(gate_sum)
    down_home = plan.collect_home(down_sum)
    back, out_back, grad_h1, bias_sum, gate_home, down_home = hold(
        back, out_back, grad_h1, bias_sum, gate_home, down_home
    )

    def along_tp(own, steps):
        pieces = {0: own}
        for mask in steps:
            for k in sorted(pieces):
                pieces[k | mask] = swap(pieces[k], "tp", mask)
        return pieces

    own = plan.returned_rows(back, quarter, inputs.shape[1])
    out_own = plan.returned_rows(out_back, quarter, inputs.shape[1])
    wide_masks, core_masks = plan.tp_masks[:0:-1], plan.tp_masks[:1]
    pieces = gather(own, [("tp", m, m) for m in wide_masks])
    out_pieces = gather(out_own, [("tp", m, m) for m in wide_masks])
    sums = jnp.stack(
        [
            jnp.sum(grad_h1 * n_first, 0),
            jnp.sum(grad_h1, 0),
            jnp.sum(grad_h2 * n_second, 0),
            jnp.sum(grad_h2, 0),
        ]
    )
    for mask in core_masks:
        sums = sums + swap(sums, "tp", mask)
    grad_gate, grad_down = gate_home, down_home
    pieces, out_pieces, sums = hold(pieces, out_pieces, sums)

    def across_cores(pieces):
        keys = sorted(pieces)
        got = swap(joined([pieces[k] for k in keys]), "tp", core_masks[0])
        size = got.shape[0] // len(keys)
        pieces = {**pieces, **{k | core_masks[0]: got[i * size : (i + 1) * size] for i, k in enumerate(keys)}}
        return plan.of_tp(pieces).reshape(inputs.shape)

    input_grad = across_cores(pieces)
    layer_out = across_cores(out_pieces)
    attn_home = plan.collect_home(attn_sum)
    grad_entry = [part[:, : 3 * head_width] for part in attn_home]
    grad_output = [part[:, 3 * head_width :] for part in attn_home]

    bias_sum = jnp.sum(bias_sum[:, 0], 0)
    for mask in plan.outer:
        bias_sum = bias_sum + swap(bias_sum, "seq", mask)
    bias_sum = bias_sum.reshape(3, heads_here, HD)
    got = [bias_sum] + [swap(bias_sum, "seq", plan.inner_mask(j)) for j in range(1, parts)]
    bias_sum = joined(pick(got, plan.part_flags), 1)
    grad_bias = lax.dynamic_slice_in_dim(bias_sum, plan.seq * slim, slim, 2)
    for mask in wide_masks:
        sums = sums + swap(sums, "tp", mask)
    sums = plan.restored(sums)
    for mask in seq_masks:
        sums = sums + swap(sums, "seq", mask)
    slim = norm_params.shape[1]
    grad_norm = lax.dynamic_slice_in_dim(sums, plan.seq * slim, slim, 1)

    def ordered_as(grad, *order):
        return with_layout_constraint(grad, Layout(order))

    reduced = (
        grad_norm,
        ordered_as(
            joined([part.reshape(part.shape[0], 3, head_width) for part in grad_entry], -1), 1, 0, 2
        ),
        grad_bias,
        ordered_as(joined(grad_output, -1), 0, 1),
        ordered_as(
            joined([part.reshape(part.shape[0], 2, hidden) for part in grad_gate], -1), 0, 1, 2
        ),
        ordered_as(joined(grad_down, -1), 0, 1),
    )
    masters = (norm_params, entry_weight, entry_bias, output_weight, gate_weight, down_weight)
    moments = (moment_norm, moment_entry, moment_bias, moment_output, moment_gate, moment_down)
    averages = (
        average_norm,
        average_entry,
        average_bias,
        average_output,
        average_gate,
        average_down,
    )
    beta = min(0.999, (1 + STEP) / (10 + STEP))
    news, new_weights, smooths, copies = ([], [], [], [])
    for index in range(6):
        grad = reduced[index] + decays[index] * masters[index]
        moment = 0.9 * moments[index] + grad
        weight = masters[index] - rates[index] * (grad + 0.9 * moment)
        news.append(moment)
        new_weights.append(weight)
        smooths.append(beta * averages[index] + (1.0 - beta) * weight)
        copies.append(weight.astype(bf16))
    return (layer_out, input_grad, *news, *new_weights, *smooths, *copies)


def solution(mesh):
    in_specs = (
        P("seq", None, None),
        P("seq", None, None),
        P(),
        P(None, "seq"),
        P("seq", None, "tp"),
        P(None, "tp", "seq"),
        P("seq", "tp"),
        P("seq", None, "tp"),
        P("seq", "tp"),
        P(None, "seq"),
        P("seq", None, "tp"),
        P(None, "tp", "seq"),
        P("seq", "tp"),
        P("seq", None, "tp"),
        P("seq", "tp"),
        P(None, "seq"),
        P("seq", None, "tp"),
        P(None, "tp", "seq"),
        P("seq", "tp"),
        P("seq", None, "tp"),
        P("seq", "tp"),
    )
    out_specs = (
        P("seq", None, None),
        P("seq", None, None),
        P(None, "seq"),
        P("seq", None, "tp"),
        P(None, "tp", "seq"),
        P("seq", "tp"),
        P("seq", None, "tp"),
        P("seq", "tp"),
        P(None, "seq"),
        P("seq", None, "tp"),
        P(None, "tp", "seq"),
        P("seq", "tp"),
        P("seq", None, "tp"),
        P("seq", "tp"),
        P(None, "seq"),
        P("seq", None, "tp"),
        P(None, "tp", "seq"),
        P("seq", "tp"),
        P("seq", None, "tp"),
        P("seq", "tp"),
        P(None, "seq"),
        P("seq", None, "tp"),
        P(None, "tp", "seq"),
        P("seq", "tp"),
        P("seq", None, "tp"),
        P("seq", "tp"),
    )
    return jax.shard_map(body, mesh=mesh, in_specs=in_specs, out_specs=out_specs, check_vma=False)
```

```python
import numpy as np

import jax
import jax.numpy as jnp
from jax import lax
from jax.experimental import pallas as pl
from jax.experimental.layout import Layout, with_layout_constraint
from jax.experimental.pallas import tpu as pltpu
from jax.sharding import PartitionSpec as P

HD = 64
ROT = 16
STEP = 10

eps = 1e-05
rates = (0.0005, 0.0002, 0.0025, 0.004, 0.0002, 6e-05)
decays = (0.0, 0.0001, 0.0, 0.0001, 0.0001, 0.0001)
bf16 = jnp.bfloat16
f32 = jnp.float32


def swap(array, axis, mask):
    pairs = [(i, i ^ mask) for i in range(lax.axis_size(axis))]
    return lax.ppermute(array, axis, pairs)


def pick(parts, flags):
    count = len(parts)
    for place, flag in enumerate(flags):
        bit = count >> (place + 1)
        parts = [jnp.where(flag, parts[j ^ bit], parts[j]) for j in range(count)]
    return parts


def joined(parts, axis=0):
    return parts[0] if len(parts) == 1 else jnp.concatenate(parts, axis)


def gather(piece, steps):
    pieces = {0: piece}
    rows = piece.shape[0]
    for axis, mask, bit in steps:
        keys = sorted(pieces)
        got = swap(joined([pieces[k] for k in keys]), axis, mask)
        for place, k in enumerate(keys):
            pieces[k | bit] = got[place * rows : (place + 1) * rows]
    return pieces


def scatter(pieces, steps):
    for axis, mask, bit in steps:
        keys = sorted(k for k in pieces if k & bit)
        got = swap(joined([pieces[k].astype(bf16) for k in keys]), axis, mask)
        rows = got.shape[0] // len(keys)
        kept = {k: v for k, v in pieces.items() if not k & bit}
        for place, k in enumerate(keys):
            kept[k ^ bit] = kept[k ^ bit].astype(f32) + got[place * rows : (place + 1) * rows].astype(f32)
        pieces = kept
    return pieces[0]


def added(near, start, stop):
    return near[0][start:stop] + near[1][start:stop].astype(f32)


class Plan:
    def __init__(self, rows):
        self.n_seq = lax.axis_size("seq")
        self.n_tp = lax.axis_size("tp")
        self.seq = lax.axis_index("seq")
        self.tp = lax.axis_index("tp")
        bits = self.n_seq.bit_length() - 1
        self.inner = [1 << i for i in range(bits // 2)][::-1]
        self.outer = [1 << i for i in range(bits) if (1 << i) not in self.inner][::-1]
        self.groups = 1 << len(self.outer)
        self.parts = 1 << len(self.inner)
        self.rows = rows // self.groups
        self.group_flags = [(self.seq & m) != 0 for m in self.outer]
        self.part_flags = [(self.seq & m) != 0 for m in self.inner]
        self.tp_masks = [1 << i for i in range(self.n_tp.bit_length() - 1)]
        self.tp_flags = [(self.tp & m) != 0 for m in self.tp_masks[::-1]]
        self.group = self.index(self.group_flags)
        order = [("tp", m) for m in self.tp_masks] + [("seq", m) for m in self.inner]
        self.members = 1 << len(order)
        self.steps = [(axis, mask, self.members >> (i + 1)) for i, (axis, mask) in enumerate(order)]
        self.group_steps = [("seq", m, self.groups >> (i + 1)) for i, m in enumerate(self.outer)]

    def index(self, flags):
        value = jnp.int32(0)
        for flag in flags:
            value = value * 2 + flag.astype(jnp.int32)
        return value

    def outer_mask(self, j):
        return sum(m for i, m in enumerate(self.outer) if j & (self.groups >> (i + 1)))

    def inner_mask(self, j):
        return sum(m for i, m in enumerate(self.inner) if j & (self.parts >> (i + 1)))

    def member_masks(self, k):
        seq = sum(m for a, m, bit in self.steps if a == "seq" and k & bit)
        tp = sum(m for a, m, bit in self.steps if a == "tp" and k & bit)
        return seq, tp

    def arranged(self, array):
        wide = array.shape[-1] // self.n_seq
        places = [self.outer_mask(g) | self.inner_mask(h) for g in range(self.groups) for h in range(self.parts)]
        return joined([array[..., p * wide : (p + 1) * wide] for p in places], -1)

    def restored(self, array):
        wide = array.shape[-1] // self.n_seq
        blocks = [None] * self.n_seq
        for g in range(self.groups):
            for h in range(self.parts):
                at = g * self.parts + h
                blocks[self.outer_mask(g) | self.inner_mask(h)] = array[..., at * wide : (at + 1) * wide]
        return joined(blocks, -1)

    def lists(self):
        return [
            [self.outer_mask(g) | self.inner_mask(h) for g in range(self.groups)] for h in range(self.parts)
        ]

    def chosen(self, j, part, all_rows):
        row = lax.broadcasted_iota(jnp.int32, (self.rows * part, part * all_rows), 0)
        column = lax.broadcasted_iota(jnp.int32, (self.rows * part, part * all_rows), 1)
        source = (row % part) * all_rows + (self.group ^ j) * self.rows + row // part
        return (column == source).astype(bf16)

    def outgoing_rows(self, array):
        block, all_rows, width = array.shape
        part = block // self.n_tp
        size = part * all_rows
        own = lax.dynamic_slice_in_dim(array.reshape(-1, width), self.tp * size, size, 0)
        return [
            jnp.dot(self.chosen(j, part, all_rows), own, preferred_element_type=f32).astype(bf16)
            for j in range(self.groups)
        ]

    def over_groups(self, pieces):
        return [swap(piece, "seq", self.outer_mask(j)) if j else piece for j, piece in enumerate(pieces)]

    def returning_rows(self, tokens):
        table = self.restored(tokens)
        size = table.shape[0] // self.groups
        return [table[j * size : (j + 1) * size] for j in range(self.groups)]

    def returned_rows(self, got, part, all_rows):
        back = jnp.concatenate([self.chosen(j, part, all_rows) for j in range(self.groups)], 0)
        return jnp.einsum("sp,sd->pd", back, jnp.concatenate(got, 0), preferred_element_type=f32).astype(bf16)

    def of_tp(self, pieces):
        return joined(pick([pieces[k] for k in range(self.n_tp)], self.tp_flags), 0)

    def chips_sides(self, piece):
        far = self.steps[1:]
        if len(far) != 2:
            return gather(piece, far)
        return [swap(piece, axis, mask) for axis, mask, _ in far]

    def chips_corner(self, piece, sides):
        far = self.steps[1:]
        if len(far) != 2:
            return sides
        half = piece.shape[0] // 2
        (axis_x, mask_x, _), (axis_z, mask_z, _) = far
        return [swap(sides[0][:half], axis_z, mask_z), swap(sides[1][half:], axis_x, mask_x)]

    def chips_near(self, piece, sides, corner):
        if len(self.steps) != 3:
            return joined([sides[k] for k in sorted(sides)])
        return jnp.concatenate([piece, sides[1], sides[0], corner[0], corner[1]], 0)

    def swap_core(self, array):
        axis, mask, _ = self.steps[0]
        return swap(array, axis, mask)

    def sum_corner(self, near):
        far = self.steps[1:]
        rows = near[0].shape[0] >> len(far)
        if len(far) != 2:
            return [scatter({k: added(near, k * rows, (k + 1) * rows) for k in range(1 << len(far))}, far)]
        (axis_x, mask_x, _), (axis_z, mask_z, _) = far
        middle = 3 * rows + rows // 2
        one = added(near, 3 * rows, middle).astype(bf16)
        two = added(near, middle, 4 * rows).astype(bf16)
        return [swap(one, axis_x, mask_x), swap(two, axis_z, mask_z)]

    def sum_sides(self, near, corner):
        far = self.steps[1:]
        if len(far) != 2:
            return corner
        (axis_x, mask_x, _), (axis_z, mask_z, _) = far
        rows = near[0].shape[0] // 4
        half = rows // 2
        one, two = added(near, rows, 2 * rows), added(near, 2 * rows, 3 * rows)
        for_z = jnp.concatenate([one[:half] + corner[0].astype(f32), one[half:]], 0).astype(bf16)
        for_x = jnp.concatenate([two[:half], two[half:] + corner[1].astype(f32)], 0).astype(bf16)
        return [swap(for_z, axis_z, mask_z), swap(for_x, axis_x, mask_x)]

    def sum_end(self, near, sides):
        if len(self.steps) != 3:
            return sides[0]
        rows = near[0].shape[0] // 4
        return added(near, 0, rows) + sides[0].astype(f32) + sides[1].astype(f32)

    def spread_mine(self, mine, axis):
        got = [mine[0]] + [swap(mine[j], "seq", self.inner_mask(j)) for j in range(1, self.parts)]
        return joined(pick(got, self.part_flags), axis)

    def collect_home(self, block_sum):
        rows = block_sum.shape[0] // self.parts
        blocks = [block_sum[h * rows : (h + 1) * rows] for h in range(self.parts)]
        mine = pick(blocks, self.part_flags)
        got = [mine[0].astype(f32)] + [
            swap(mine[j].astype(bf16), "seq", self.inner_mask(j)).astype(f32) for j in range(1, self.parts)
        ]
        return pick(got, self.part_flags)

    def all_blocks(self, block):
        return lax.all_gather(block, "seq", axis_index_groups=self.lists(), axis=0, tiled=True)

    def sum_blocks(self, product):
        return lax.psum_scatter(
            product, "seq", scatter_dimension=0, axis_index_groups=self.lists(), tiled=True
        )


def hold(*values):
    return lax.optimization_barrier(values)


def layer_norm(values, gain, shift):
    center = values - jnp.mean(values, -1, keepdims=True)
    var = jnp.mean(center * center, -1, keepdims=True)
    inverse = lax.rsqrt(var + eps)
    normed = center * inverse
    return (normed * gain + shift, normed, inverse)


def norm_back(grad, normed, inverse, gain):
    scaled = grad * gain
    inner = (
        scaled
        - jnp.mean(scaled, -1, keepdims=True)
        - normed * jnp.mean(scaled * normed, -1, keepdims=True)
    )
    return inner * inverse


def turning(position):
    lane = jnp.arange(128, dtype=jnp.int32) % HD
    half = ROT // 2
    freq = 10000.0 ** (-(lane % half).astype(f32) / half)
    angle = position.astype(f32)[:, None] * jnp.where(lane < ROT, freq, 0.0)[None, :]
    return jnp.cos(angle), jnp.sin(angle) * jnp.where(lane < half, -1.0, 1.0)[None, :]


def turned(values, cosine, sine):
    wide = values.shape[1]
    half = ROT // 2
    lane = lax.broadcasted_iota(jnp.int32, values.shape, 1) & (HD - 1)
    partner = jnp.where(lane < half, pltpu.roll(values, wide - half, 1), pltpu.roll(values, half, 1))
    return values * cosine + partner * sine


def widened(table, wide):
    return table if wide == table.shape[1] else jnp.concatenate([table] * (wide // table.shape[1]), 1)


def head_lanes(shape, head):
    return lax.broadcasted_iota(jnp.int32, shape, len(shape) - 1) // HD == head


def dot(left, right, over):
    return lax.dot_general(left, right, (over, ((), ())), preferred_element_type=f32)


def forward_kernel(lens, mixed, shift, cosine, sine, column, line, qkv_ref, low_ref, full_ref, sums_ref):
    wide = mixed.shape[-1] // 3
    length = line.shape[1]
    values = mixed[...].reshape(length, 3 * wide) + shift[...]
    cos, sin = widened(cosine[...], wide), widened(sine[...], wide)
    query = (turned(values[:, :wide], cos, sin) * 0.125).astype(bf16)
    keys = turned(values[:, wide : 2 * wide], cos, sin).astype(bf16)
    vals = values[:, 2 * wide :].astype(bf16)
    for place, part in enumerate((query, keys, vals)):
        qkv_ref[:, :, :, place * wide : (place + 1) * wide] = part.reshape(qkv_ref.shape[:-1] + (wide,))
    size = min(512, length)
    blocks = mixed.shape[0] * size // length
    limit = lens[pl.program_id(0)]
    for start in range(0, length, size):
        rows = slice(start, start + size)
        valid = (line[...] <= column[rows]) & (line[...] < limit)
        out = jnp.zeros((size, wide), f32)
        kept = jnp.zeros((size, 128), f32)
        for head in range(wide // HD):
            here = head_lanes((size, wide), head)
            scores = dot(jnp.where(here, query[rows], 0), keys, ((1,), (1,)))
            scores = jnp.where(valid, scores, -1e30)
            top = jnp.max(scores, 1, keepdims=True)
            weights = jnp.exp(scores - top)
            total = jnp.sum(weights, 1, keepdims=True)
            probs = (weights * (1.0 / total)).astype(bf16)
            out = jnp.where(here, dot(probs, vals, ((1,), (0,))), out)
            lane = lax.broadcasted_iota(jnp.int32, kept.shape, 1)
            kept = jnp.where(lane == head, top + jnp.log(total), kept)
        at = slice(start // size * blocks, (start // size + 1) * blocks)
        low_ref[at] = out.astype(bf16).reshape((blocks,) + low_ref.shape[1:])
        full_ref[at] = out.reshape((blocks,) + full_ref.shape[1:])
        sums_ref[0, rows] = kept


def backward_kernel(lens, qkv, grad, full, sums, cosine, sine, column, line, out_ref, bias_ref):
    wide = grad.shape[-1]
    length = line.shape[1]
    values = qkv[...].reshape(length, 3 * wide)
    query, keys, vals = (values[:, i * wide : (i + 1) * wide] for i in range(3))
    grads = grad[...].reshape(length, wide)
    attended = full[...].reshape(length, wide)
    size = min(512, length)
    limit = lens[pl.program_id(0)]
    grad_query = []
    grad_key = jnp.zeros((length, wide), f32)
    grad_val = jnp.zeros((length, wide), f32)
    for start in range(0, length, size):
        rows = slice(start, start + size)
        valid = (line[...] <= column[rows]) & (line[...] < limit)
        both = grads[rows].astype(f32) * attended[rows]
        grad_here = jnp.zeros((size, wide), f32)
        for head in range(wide // HD):
            here = head_lanes((size, wide), head)
            own_query = jnp.where(here, query[rows], 0)
            own_grad = jnp.where(here, grads[rows], 0)
            own_keys = jnp.where(head_lanes((length, wide), head), keys, 0)
            delta = jnp.sum(jnp.where(here, both, 0.0), 1, keepdims=True)
            scores = dot(own_query, keys, ((1,), (1,)))
            probs = jnp.where(valid, jnp.exp(scores - sums[0, rows, head : head + 1]), 0.0)
            grad_val = grad_val + dot(probs.astype(bf16), own_grad, ((0,), (0,)))
            grad_prob = dot(own_grad, vals, ((1,), (1,)))
            grad_score = (probs * (grad_prob - delta)).astype(bf16)
            grad_here = grad_here + dot(grad_score, own_keys, ((1,), (0,)))
            grad_key = grad_key + dot(grad_score, own_query, ((0,), (0,)))
        grad_query.append(grad_here)
    cos, sin = widened(cosine[...], wide), -widened(sine[...], wide)
    grad_query = turned(joined(grad_query) * 0.125, cos, sin)
    grad_key = turned(grad_key, cos, sin)
    for place, part in enumerate((grad_query, grad_key, grad_val)):
        part = part.astype(bf16)
        at = slice(place * wide, (place + 1) * wide)
        out_ref[:, :, :, at] = part.reshape(out_ref.shape[:-1] + (wide,))
        bias_ref[0, :, at] = jnp.broadcast_to(jnp.sum(part.astype(f32), 0, keepdims=True), (8, wide))


def of_row(array):
    blocks, _, places, wide = array.shape
    return pl.BlockSpec((blocks, 1, places, wide), lambda r, lens: (0, r, 0, 0))


def entire(array):
    return pl.BlockSpec(array.shape, lambda r, lens: (0,) * array.ndim)


def attend_forward(mixed, shift, tables, lens):
    blocks, rows, places, wide = mixed.shape
    wide = wide // 3
    length = blocks * places
    out = [
        jax.ShapeDtypeStruct((blocks, rows, places, 3 * wide), bf16),
        jax.ShapeDtypeStruct((blocks, rows, places, wide), bf16),
        jax.ShapeDtypeStruct((blocks, rows, places, wide), f32),
        jax.ShapeDtypeStruct((rows, length, 128), f32),
    ]
    return pl.pallas_call(
        forward_kernel,
        out_shape=out,
        grid_spec=pltpu.PrefetchScalarGridSpec(
            num_scalar_prefetch=1,
            grid=(rows,),
            in_specs=[of_row(mixed), entire(shift)] + [entire(t) for t in tables],
            out_specs=[of_row(o) for o in out[:3]]
            + [pl.BlockSpec((1, length, 128), lambda r, lens: (r, 0, 0))],
        ),
        compiler_params=pltpu.CompilerParams(vmem_limit_bytes=40 << 20),
        name="attend_forward",
    )(lens, mixed, shift, *tables)


def attend_backward(qkv, grad, full, sums, tables, lens):
    blocks, rows, places, wide = grad.shape
    length = blocks * places
    out = [
        jax.ShapeDtypeStruct(qkv.shape, bf16),
        jax.ShapeDtypeStruct((rows, 8, 3 * wide), f32),
    ]
    return pl.pallas_call(
        backward_kernel,
        out_shape=out,
        grid_spec=pltpu.PrefetchScalarGridSpec(
            num_scalar_prefetch=1,
            grid=(rows,),
            in_specs=[
                of_row(qkv),
                of_row(grad),
                of_row(full),
                pl.BlockSpec((1, length, 128), lambda r, lens: (r, 0, 0)),
            ]
            + [entire(t) for t in tables],
            out_specs=[of_row(out[0]), pl.BlockSpec((1, 8, 3 * wide), lambda r, lens: (r, 0, 0))],
        ),
        compiler_params=pltpu.CompilerParams(vmem_limit_bytes=48 << 20),
        name="attend_backward",
    )(lens, qkv, grad, full, sums, *tables)


def body(
    inputs,
    cotangent,
    lengths,
    norm_params,
    entry_weight,
    entry_bias,
    output_weight,
    gate_weight,
    down_weight,
    moment_norm,
    moment_entry,
    moment_bias,
    moment_output,
    moment_gate,
    moment_down,
    average_norm,
    average_entry,
    average_bias,
    average_output,
    average_gate,
    average_down,
):
    plan = Plan(inputs.shape[1])
    gate_master, down_master = gate_weight, down_weight
    groups, parts, rows = plan.groups, plan.parts, plan.rows
    block_len, _, width = inputs.shape
    tp_width = entry_weight.shape[2]
    head_width = tp_width // parts
    heads_here = head_width // HD
    hidden = gate_weight.shape[2] // parts
    quarter = block_len // plan.n_tp
    share = rows * groups * quarter
    plan.total = share * plan.members
    length = block_len * plan.n_seq

    member_seq = np.array([plan.member_masks(k)[0] for k in range(plan.members)], np.int32)
    member_tp = np.array([plan.member_masks(k)[1] for k in range(plan.members)], np.int32)
    sender = np.array([plan.outer_mask(j) for j in range(groups)], np.int32)
    seq_at = plan.seq ^ (member_seq[:, None] | sender[None, :])
    tp_at = plan.tp ^ member_tp
    position = (
        (seq_at * block_len)[:, :, None]
        + (tp_at * quarter)[:, None, None]
        + np.arange(quarter, dtype=np.int32)[None, None, :]
    )
    lens = lax.dynamic_slice_in_dim(lengths, plan.group * rows, rows, 0)

    def over_masks(array, masks):
        sums = [0]
        for mask in masks:
            sums = sums + [m | mask for m in sums]
        return [swap(array, "seq", m) for m in sums[1:]]

    def total_of(array, got):
        for other in got:
            array = array + other
        return array

    lane_block = lax.broadcasted_iota(jnp.int32, (4, width), 1) // norm_params.shape[1]
    small = jnp.where(lane_block == plan.seq, jnp.tile(norm_params.astype(bf16), (1, plan.n_seq)), 0)
    slim = entry_bias.shape[2]
    slot = lax.broadcasted_iota(jnp.int32, (slim, HD), 1) == plan.seq * slim + lax.broadcasted_iota(
        jnp.int32, (slim, HD), 0
    )
    placed = jnp.dot(entry_bias.reshape(-1, slim).astype(bf16), slot.astype(bf16), preferred_element_type=f32)
    placed = placed.astype(bf16).reshape(1, 3 * tp_width)
    placed = jnp.pad(placed, ((0, 0), (0, width - 3 * tp_width)))
    small = jnp.concatenate([small, placed], 0)
    seq_masks = [1 << i for i in range(plan.n_seq.bit_length() - 1)]
    last_mask = plan.outer[-1]
    first_masks = [m for m in seq_masks if m != last_mask]

    def columns(array, h, size):
        return array[..., h * size : (h + 1) * size].astype(bf16).reshape(array.shape[0], -1)

    def turned_columns(array, h):
        return array[:, h * hidden : (h + 1) * hidden].astype(bf16).T

    attn_mine = pick(
        [
            jnp.concatenate(
                [columns(entry_weight, h, head_width), columns(output_weight, h, head_width)], 1
            )
            for h in range(parts)
        ],
        plan.part_flags,
    )
    attn_block = plan.spread_mine(attn_mine, 0)
    outgoing = plan.outgoing_rows(inputs)
    attn_block, outgoing, small, gate_weight, down_weight, cotangent, position = hold(
        attn_block, outgoing, small, gate_weight, down_weight, cotangent, position
    )

    w_attn = plan.all_blocks(attn_block)
    small_got = over_masks(small, first_masks)
    resid = plan.over_groups(outgoing)
    gate_mine = pick([columns(gate_weight, h, hidden) for h in range(parts)], plan.part_flags)
    gate_block = plan.spread_mine(gate_mine, 0)
    small, small_got, resid, gate_block, cotangent, down_weight, position = hold(
        small, small_got, resid, gate_block, cotangent, down_weight, position
    )

    small = total_of(small, small_got)
    small_got = over_masks(small, [last_mask])
    down_mine = pick([columns(down_weight, h, hidden) for h in range(parts)], plan.part_flags)
    down_block = plan.spread_mine(down_mine, 0)
    small, small_got, down_block, gate_block, cotangent = hold(
        small, small_got, down_block, gate_block, cotangent
    )

    small = total_of(small, small_got)
    gains = plan.arranged(small[:4]).astype(f32)
    resid = plan.arranged(jnp.concatenate(resid, 0)).astype(f32)
    h_first, n_first, i_first = layer_norm(resid, gains[0], gains[1])
    low_first = h_first.astype(bf16)
    sides = plan.chips_sides(low_first)
    row_position = position.reshape(length)
    tables = turning(row_position) + (row_position[:, None], row_position[None, :])
    blank = jnp.zeros((down_block.shape[0], -(2 * hidden + hidden) % 128), bf16)
    ffn_block = jnp.concatenate([gate_block, down_block, blank], 1)
    low_first, sides, tables, ffn_block, cotangent = hold(low_first, sides, tables, ffn_block, cotangent)
    corner = plan.chips_corner(low_first, sides)
    outgoing = plan.outgoing_rows(cotangent)
    low_first, sides, corner, outgoing = hold(low_first, sides, corner, outgoing)
    near = plan.chips_near(low_first, sides, corner)
    other = plan.swap_core(near)
    a_first = jnp.concatenate([near, other], 0)
    a_first, w_attn, ffn_block, outgoing = hold(a_first, w_attn, ffn_block, outgoing)
    w_ffn = plan.all_blocks(ffn_block)
    grad_y = plan.over_groups(outgoing)
    own_position = jnp.broadcast_to(position[0][:, None, :], (groups, rows, quarter))
    real = (own_position < lens[None, :, None]).reshape(share, 1)

    w_entry = w_attn[:, : 3 * head_width]
    w_output = w_attn[:, 3 * head_width :]
    mixed = jnp.einsum("td,df->tf", a_first, w_entry, preferred_element_type=f32)
    mixed = mixed.reshape(plan.members * groups, rows, quarter, 3 * head_width)
    biases = [
        jnp.concatenate(
            [
                small[4:, c * tp_width + h * head_width : c * tp_width + (h + 1) * head_width]
                for c in range(3)
            ],
            1,
        )
        for h in range(parts)
    ]
    entry_shift = pick(biases, plan.part_flags)[0].astype(f32)
    qkv, att_low, attended, score_sums = attend_forward(mixed, entry_shift, tables, lens)
    att_low = att_low.reshape(plan.total, head_width)

    def output_product(lo, hi):
        return jnp.einsum("th,dh->td", att_low[lo:hi], w_output, preferred_element_type=f32)

    half = plan.total // 2
    far_product = output_product(half, plan.total).astype(bf16)
    far_product, grad_y = hold(far_product, grad_y)

    got = plan.swap_core(far_product)
    product = output_product(0, half)
    grad_y = plan.arranged(jnp.concatenate(grad_y, 0))
    grad_y = jnp.where(real, grad_y, 0)
    product, got, grad_y = hold(product, got, grad_y)

    near = (product, got)
    corner = plan.sum_corner(near)
    y_sides = plan.chips_sides(grad_y)
    near, corner, y_sides = hold(near, corner, y_sides)
    sides = plan.sum_sides(near, corner)
    y_corner = plan.chips_corner(grad_y, y_sides)
    near, sides, y_corner = hold(near, sides, y_corner)

    second = resid + plan.sum_end(near, sides)
    h_second, n_second, i_second = layer_norm(second, gains[2], gains[3])
    low_second = h_second.astype(bf16)
    sides = plan.chips_sides(low_second)
    y_near = plan.chips_near(grad_y, y_sides, y_corner)
    y_other = plan.swap_core(y_near)
    second, low_second, sides, y_near, y_other = hold(second, low_second, sides, y_near, y_other)
    corner = plan.chips_corner(low_second, sides)
    grad_y_all = jnp.concatenate([y_near, y_other], 0)
    low_second, sides, corner, grad_y_all = hold(low_second, sides, corner, grad_y_all)
    near = plan.chips_near(low_second, sides, corner)
    other = plan.swap_core(near)
    a_second = jnp.concatenate([near, other], 0)
    a_second, w_ffn = hold(a_second, w_ffn)

    w_gate = w_ffn[:, : 2 * hidden]
    gated = jnp.einsum("td,df->tf", a_second, w_gate, preferred_element_type=f32)
    gate = gated[:, :hidden]
    upper = gated[:, hidden:]
    sigma = jax.nn.sigmoid(gate)
    active_gate = gate * sigma
    hid = (active_gate * upper).astype(bf16)
    grad_down = jnp.einsum("td,tf->df", grad_y_all, hid, preferred_element_type=f32).astype(bf16)
    hid, grad_down, w_ffn = hold(hid, grad_down, w_ffn)
    w_down = w_ffn[:, 2 * hidden : 3 * hidden]
    down_sum = plan.sum_blocks(grad_down)
    grad_hidden = jnp.einsum(
        "td,df->tf", grad_y_all, w_down, preferred_element_type=f32
    ).astype(bf16)
    grad_gate_val = grad_hidden * upper * (sigma * (1.0 + gate * (1.0 - sigma)))
    grad_up_val = grad_hidden * active_gate
    grad_gated = jnp.concatenate([grad_gate_val, grad_up_val], 1).astype(bf16)

    def gate_product(lo, hi):
        return jnp.einsum("tf,df->td", grad_gated[lo:hi], w_gate, preferred_element_type=f32)

    def down_product(lo, hi):
        return jnp.einsum("tf,df->td", hid[lo:hi], w_down, preferred_element_type=f32)

    far_product = gate_product(half, plan.total).astype(bf16)
    hid, grad_gated, far_product = hold(hid, grad_gated, far_product)

    got = plan.swap_core(far_product)
    product = gate_product(0, half)
    grad_gate = jnp.einsum("td,tf->df", a_second, grad_gated, preferred_element_type=f32).astype(bf16)
    product, got, hid, grad_gate, down_sum = hold(product, got, hid, grad_gate, down_sum)
    gate_sum = plan.sum_blocks(grad_gate)

    near = (product, got)
    corner = plan.sum_corner(near)
    near, corner, hid, down_sum = hold(near, corner, hid, down_sum)
    sides = plan.sum_sides(near, corner)
    out_far = down_product(half, plan.total).astype(bf16)
    near, sides, out_far, hid, down_sum = hold(near, sides, out_far, hid, down_sum)

    out_got = plan.swap_core(out_far)
    grad_h2 = plan.sum_end(near, sides)
    grad_second = grad_y.astype(f32) + norm_back(grad_h2, n_second, i_second, gains[2])
    low_grad = grad_second.astype(bf16)
    sides = plan.chips_sides(low_grad)
    out_near = down_product(0, half)
    low_grad, sides, out_near, out_got, grad_h2, grad_second = hold(
        low_grad, sides, out_near, out_got, grad_h2, grad_second
    )
    out_near = (out_near, out_got)
    corner = plan.chips_corner(low_grad, sides)
    out_corner = plan.sum_corner(out_near)
    low_grad, sides, corner, out_corner, out_near = hold(low_grad, sides, corner, out_corner, out_near)

    near = plan.chips_near(low_grad, sides, corner)
    other = plan.swap_core(near)
    near, other = hold(near, other)
    grad_second_all = jnp.concatenate([near, other], 0)
    grad_att = jnp.einsum(
        "td,dh->th", grad_second_all, w_output, preferred_element_type=f32
    ).astype(bf16)
    grad_att = grad_att.reshape(attended.shape)
    grad_mixed, bias_sum = attend_backward(qkv, grad_att, attended, score_sums, tables, lens)
    grad_mixed = grad_mixed.reshape(plan.total, 3 * head_width)

    def entry_product(lo, hi):
        return jnp.einsum("tf,df->td", grad_mixed[lo:hi], w_entry, preferred_element_type=f32)

    far_product = entry_product(half, plan.total).astype(bf16)
    out_sides = plan.sum_sides(out_near, out_corner)
    far_product, grad_mixed, bias_sum, out_sides, out_near = hold(
        far_product, grad_mixed, bias_sum, out_sides, out_near
    )

    got = plan.swap_core(far_product)
    product = entry_product(0, half)
    grad_attn = jnp.concatenate(
        [
            jnp.einsum("td,tf->df", a_first, grad_mixed, preferred_element_type=f32).astype(bf16),
            jnp.einsum("td,tf->df", grad_second_all, att_low, preferred_element_type=f32).astype(bf16),
        ],
        1,
    )
    bias_sum = jnp.sum(bias_sum[:, 0], 0, keepdims=True)
    bias_got = over_masks(bias_sum, plan.outer)
    result = second + plan.sum_end(out_near, out_sides)
    out_returning = plan.returning_rows(result.astype(bf16))
    product, got, grad_attn, bias_sum, bias_got, down_sum, out_returning, gate_sum = hold(
        product, got, grad_attn, bias_sum, bias_got, down_sum, out_returning, gate_sum
    )
    attn_sum = plan.sum_blocks(grad_attn)

    bias_sum = total_of(bias_sum, bias_got)
    near = (product, got)
    corner = plan.sum_corner(near)
    bias_got = [swap(bias_sum, "seq", plan.inner_mask(j)) for j in range(1, parts)]
    near, corner, bias_sum, bias_got, down_sum, gate_sum, out_returning = hold(
        near, corner, bias_sum, bias_got, down_sum, gate_sum, out_returning
    )
    sides = plan.sum_sides(near, corner)
    out_back = plan.over_groups(out_returning)
    near, sides, out_back, down_sum, gate_sum = hold(near, sides, out_back, down_sum, gate_sum)

    def along_tp(own):
        return gather(own, [("tp", m, m) for m in plan.tp_masks[:0:-1]])

    grad_h1 = plan.sum_end(near, sides)
    grad_input = grad_second + norm_back(grad_h1, n_first, i_first, gains[0])
    back = plan.over_groups(plan.returning_rows(grad_input.astype(bf16)))
    grad_gate = plan.collect_home(gate_sum)
    grad_down = plan.collect_home(down_sum)
    out_pieces = along_tp(plan.returned_rows(out_back, quarter, inputs.shape[1]))
    sums = jnp.stack(
        [
            jnp.sum(grad_h1 * n_first, 0),
            jnp.sum(grad_h1, 0),
            jnp.sum(grad_h2 * n_second, 0),
            jnp.sum(grad_h2, 0),
        ]
    )
    back, grad_gate, grad_down, out_pieces, sums = hold(back, grad_gate, grad_down, out_pieces, sums)

    def ordered_as(grad, *order):
        return with_layout_constraint(grad, Layout(order))

    beta = min(0.999, (1 + STEP) / (10 + STEP))

    def stepped(index, grad, master, moment, average):
        grad = grad + decays[index] * master
        moment = 0.9 * moment + grad
        weight = master - rates[index] * (grad + 0.9 * moment)
        return moment, weight, beta * average + (1.0 - beta) * weight, weight.astype(bf16)

    grad_gate = ordered_as(
        joined([part.reshape(part.shape[0], 2, hidden) for part in grad_gate], -1), 0, 1, 2
    )
    gate = stepped(4, grad_gate, gate_master, moment_gate, average_gate)
    grad_down = ordered_as(joined(grad_down, -1), 0, 1)
    down = stepped(5, grad_down, down_master, moment_down, average_down)
    wide_masks, core_masks = plan.tp_masks[:0:-1], plan.tp_masks[:1]
    pieces = along_tp(plan.returned_rows(back, quarter, inputs.shape[1]))
    for mask in core_masks:
        sums = sums + swap(sums, "tp", mask)

    def across_cores(pieces):
        keys = sorted(pieces)
        got = swap(joined([pieces[k] for k in keys]), "tp", core_masks[0])
        size = got.shape[0] // len(keys)
        pieces = {**pieces, **{k | core_masks[0]: got[i * size : (i + 1) * size] for i, k in enumerate(keys)}}
        return plan.of_tp(pieces).reshape(inputs.shape)

    layer_out = across_cores(out_pieces)
    pieces, sums, layer_out, gate, down, attn_sum = hold(pieces, sums, layer_out, gate, down, attn_sum)

    input_grad = across_cores(pieces)

    got = [part.reshape(3, heads_here, HD) for part in [bias_sum] + bias_got]
    bias_sum = joined(pick(got, plan.part_flags), 1)
    grad_bias = lax.dynamic_slice_in_dim(bias_sum, plan.seq * slim, slim, 2)
    for mask in wide_masks:
        sums = sums + swap(sums, "tp", mask)
    sums = plan.restored(sums)
    for mask in seq_masks:
        sums = sums + swap(sums, "seq", mask)
    slim = norm_params.shape[1]
    grad_norm = lax.dynamic_slice_in_dim(sums, plan.seq * slim, slim, 1)

    norm = stepped(0, grad_norm, norm_params, moment_norm, average_norm)
    bias = stepped(2, grad_bias, entry_bias, moment_bias, average_bias)
    attn_home = plan.collect_home(attn_sum)
    grad_entry = [part[:, : 3 * head_width] for part in attn_home]
    grad_entry = ordered_as(
        joined([part.reshape(part.shape[0], 3, head_width) for part in grad_entry], -1), 1, 0, 2
    )
    grad_output = ordered_as(joined([part[:, 3 * head_width :] for part in attn_home], -1), 0, 1)
    entry = stepped(1, grad_entry, entry_weight, moment_entry, average_entry)
    output = stepped(3, grad_output, output_weight, moment_output, average_output)
    kinds = zip(norm, entry, bias, output, gate, down)
    return (layer_out, input_grad, *(array for kind in kinds for array in kind))


def solution(mesh):
    in_specs = (
        P("seq", None, None),
        P("seq", None, None),
        P(),
        P(None, "seq"),
        P("seq", None, "tp"),
        P(None, "tp", "seq"),
        P("seq", "tp"),
        P("seq", None, "tp"),
        P("seq", "tp"),
        P(None, "seq"),
        P("seq", None, "tp"),
        P(None, "tp", "seq"),
        P("seq", "tp"),
        P("seq", None, "tp"),
        P("seq", "tp"),
        P(None, "seq"),
        P("seq", None, "tp"),
        P(None, "tp", "seq"),
        P("seq", "tp"),
        P("seq", None, "tp"),
        P("seq", "tp"),
    )
    out_specs = (
        P("seq", None, None),
        P("seq", None, None),
        P(None, "seq"),
        P("seq", None, "tp"),
        P(None, "tp", "seq"),
        P("seq", "tp"),
        P("seq", None, "tp"),
        P("seq", "tp"),
        P(None, "seq"),
        P("seq", None, "tp"),
        P(None, "tp", "seq"),
        P("seq", "tp"),
        P("seq", None, "tp"),
        P("seq", "tp"),
        P(None, "seq"),
        P("seq", None, "tp"),
        P(None, "tp", "seq"),
        P("seq", "tp"),
        P("seq", None, "tp"),
        P("seq", "tp"),
        P(None, "seq"),
        P("seq", None, "tp"),
        P(None, "tp", "seq"),
        P("seq", "tp"),
        P("seq", None, "tp"),
        P("seq", "tp"),
    )
    return jax.shard_map(body, mesh=mesh, in_specs=in_specs, out_specs=out_specs, check_vma=False)
```

```python
import numpy as np

import jax
import jax.numpy as jnp
from jax import lax
from jax.experimental import pallas as pl
from jax.experimental.layout import Layout, with_layout_constraint
from jax.experimental.pallas import tpu as pltpu
from jax.sharding import PartitionSpec as P

HD = 64
ROT = 16
STEP = 10

eps = 1e-05
rates = (0.0005, 0.0002, 0.0025, 0.004, 0.0002, 6e-05)
decays = (0.0, 0.0001, 0.0, 0.0001, 0.0001, 0.0001)
bf16 = jnp.bfloat16
f32 = jnp.float32


def swap(array, axis, mask):
    pairs = [(i, i ^ mask) for i in range(lax.axis_size(axis))]
    return lax.ppermute(array, axis, pairs)


def pick(parts, flags):
    count = len(parts)
    for place, flag in enumerate(flags):
        bit = count >> (place + 1)
        parts = [jnp.where(flag, parts[j ^ bit], parts[j]) for j in range(count)]
    return parts


def joined(parts, axis=0):
    return parts[0] if len(parts) == 1 else jnp.concatenate(parts, axis)


def gather(piece, steps):
    pieces = {0: piece}
    rows = piece.shape[0]
    for axis, mask, bit in steps:
        keys = sorted(pieces)
        got = swap(joined([pieces[k] for k in keys]), axis, mask)
        for place, k in enumerate(keys):
            pieces[k | bit] = got[place * rows : (place + 1) * rows]
    return pieces


def scatter(pieces, steps):
    for axis, mask, bit in steps:
        keys = sorted(k for k in pieces if k & bit)
        got = swap(joined([pieces[k].astype(bf16) for k in keys]), axis, mask)
        rows = got.shape[0] // len(keys)
        kept = {k: v for k, v in pieces.items() if not k & bit}
        for place, k in enumerate(keys):
            kept[k ^ bit] = kept[k ^ bit].astype(f32) + got[place * rows : (place + 1) * rows].astype(f32)
        pieces = kept
    return pieces[0]


def added(near, start, stop):
    return near[0][start:stop] + near[1][start:stop].astype(f32)


class Plan:
    def __init__(self, rows):
        self.n_seq = lax.axis_size("seq")
        self.n_tp = lax.axis_size("tp")
        self.seq = lax.axis_index("seq")
        self.tp = lax.axis_index("tp")
        bits = self.n_seq.bit_length() - 1
        self.inner = [1 << i for i in range(bits // 2)][::-1]
        self.outer = [1 << i for i in range(bits) if (1 << i) not in self.inner][::-1]
        self.groups = 1 << len(self.outer)
        self.parts = 1 << len(self.inner)
        self.rows = rows // self.groups
        self.group_flags = [(self.seq & m) != 0 for m in self.outer]
        self.part_flags = [(self.seq & m) != 0 for m in self.inner]
        self.tp_masks = [1 << i for i in range(self.n_tp.bit_length() - 1)]
        self.tp_flags = [(self.tp & m) != 0 for m in self.tp_masks[::-1]]
        self.group = self.index(self.group_flags)
        order = [("tp", m) for m in self.tp_masks] + [("seq", m) for m in self.inner]
        self.members = 1 << len(order)
        self.steps = [(axis, mask, self.members >> (i + 1)) for i, (axis, mask) in enumerate(order)]
        self.group_steps = [("seq", m, self.groups >> (i + 1)) for i, m in enumerate(self.outer)]

    def index(self, flags):
        value = jnp.int32(0)
        for flag in flags:
            value = value * 2 + flag.astype(jnp.int32)
        return value

    def outer_mask(self, j):
        return sum(m for i, m in enumerate(self.outer) if j & (self.groups >> (i + 1)))

    def inner_mask(self, j):
        return sum(m for i, m in enumerate(self.inner) if j & (self.parts >> (i + 1)))

    def member_masks(self, k):
        seq = sum(m for a, m, bit in self.steps if a == "seq" and k & bit)
        tp = sum(m for a, m, bit in self.steps if a == "tp" and k & bit)
        return seq, tp

    def arranged(self, array):
        wide = array.shape[-1] // self.n_seq
        places = [self.outer_mask(g) | self.inner_mask(h) for g in range(self.groups) for h in range(self.parts)]
        return joined([array[..., p * wide : (p + 1) * wide] for p in places], -1)

    def restored(self, array):
        wide = array.shape[-1] // self.n_seq
        blocks = [None] * self.n_seq
        for g in range(self.groups):
            for h in range(self.parts):
                at = g * self.parts + h
                blocks[self.outer_mask(g) | self.inner_mask(h)] = array[..., at * wide : (at + 1) * wide]
        return joined(blocks, -1)

    def lists(self):
        return [
            [self.outer_mask(g) | self.inner_mask(h) for g in range(self.groups)] for h in range(self.parts)
        ]

    def chosen(self, j, part, all_rows):
        row = lax.broadcasted_iota(jnp.int32, (self.rows * part, part * all_rows), 0)
        column = lax.broadcasted_iota(jnp.int32, (self.rows * part, part * all_rows), 1)
        source = (row % part) * all_rows + (self.group ^ j) * self.rows + row // part
        return (column == source).astype(bf16)

    def outgoing_rows(self, array):
        block, all_rows, width = array.shape
        part = block // self.n_tp
        size = part * all_rows
        own = lax.dynamic_slice_in_dim(array.reshape(-1, width), self.tp * size, size, 0)
        return [
            jnp.dot(self.chosen(j, part, all_rows), own, preferred_element_type=f32).astype(bf16)
            for j in range(self.groups)
        ]

    def over_groups(self, pieces):
        return [swap(piece, "seq", self.outer_mask(j)) if j else piece for j, piece in enumerate(pieces)]

    def returning_rows(self, tokens):
        table = self.restored(tokens)
        size = table.shape[0] // self.groups
        return [table[j * size : (j + 1) * size] for j in range(self.groups)]

    def returned_rows(self, got, part, all_rows):
        back = jnp.concatenate([self.chosen(j, part, all_rows) for j in range(self.groups)], 0)
        return jnp.einsum("sp,sd->pd", back, jnp.concatenate(got, 0), preferred_element_type=f32).astype(bf16)

    def of_tp(self, pieces):
        return joined(pick([pieces[k] for k in range(self.n_tp)], self.tp_flags), 0)

    def chips_sides(self, piece):
        far = self.steps[1:]
        if len(far) != 2:
            return gather(piece, far)
        return [swap(piece, axis, mask) for axis, mask, _ in far]

    def chips_corner(self, piece, sides):
        far = self.steps[1:]
        if len(far) != 2:
            return sides
        half = piece.shape[0] // 2
        (axis_x, mask_x, _), (axis_z, mask_z, _) = far
        return [swap(sides[0][:half], axis_z, mask_z), swap(sides[1][half:], axis_x, mask_x)]

    def chips_near(self, piece, sides, corner):
        if len(self.steps) != 3:
            return joined([sides[k] for k in sorted(sides)])
        return jnp.concatenate([piece, sides[1], sides[0], corner[0], corner[1]], 0)

    def swap_core(self, array):
        axis, mask, _ = self.steps[0]
        return swap(array, axis, mask)

    def sum_corner(self, near):
        far = self.steps[1:]
        rows = near[0].shape[0] >> len(far)
        if len(far) != 2:
            return [scatter({k: added(near, k * rows, (k + 1) * rows) for k in range(1 << len(far))}, far)]
        (axis_x, mask_x, _), (axis_z, mask_z, _) = far
        middle = 3 * rows + rows // 2
        one = added(near, 3 * rows, middle).astype(bf16)
        two = added(near, middle, 4 * rows).astype(bf16)
        return [swap(one, axis_x, mask_x), swap(two, axis_z, mask_z)]

    def sum_sides(self, near, corner):
        far = self.steps[1:]
        if len(far) != 2:
            return corner
        (axis_x, mask_x, _), (axis_z, mask_z, _) = far
        rows = near[0].shape[0] // 4
        half = rows // 2
        one, two = added(near, rows, 2 * rows), added(near, 2 * rows, 3 * rows)
        for_z = jnp.concatenate([one[:half] + corner[0].astype(f32), one[half:]], 0).astype(bf16)
        for_x = jnp.concatenate([two[:half], two[half:] + corner[1].astype(f32)], 0).astype(bf16)
        return [swap(for_z, axis_z, mask_z), swap(for_x, axis_x, mask_x)]

    def sum_end(self, near, sides):
        if len(self.steps) != 3:
            return sides[0]
        rows = near[0].shape[0] // 4
        return added(near, 0, rows) + sides[0].astype(f32) + sides[1].astype(f32)

    def spread_mine(self, mine, axis):
        got = [mine[0]] + [swap(mine[j], "seq", self.inner_mask(j)) for j in range(1, self.parts)]
        return joined(pick(got, self.part_flags), axis)

    def collect_home(self, block_sum):
        rows = block_sum.shape[0] // self.parts
        blocks = [block_sum[h * rows : (h + 1) * rows] for h in range(self.parts)]
        mine = pick(blocks, self.part_flags)
        got = [mine[0].astype(f32)] + [
            swap(mine[j].astype(bf16), "seq", self.inner_mask(j)).astype(f32) for j in range(1, self.parts)
        ]
        return pick(got, self.part_flags)

    def all_blocks(self, block):
        return lax.all_gather(block, "seq", axis_index_groups=self.lists(), axis=0, tiled=True)

    def sum_blocks(self, product):
        return lax.psum_scatter(
            product, "seq", scatter_dimension=0, axis_index_groups=self.lists(), tiled=True
        )


def hold(*values):
    return lax.optimization_barrier(values)


def layer_norm(values, gain, shift):
    center = values - jnp.mean(values, -1, keepdims=True)
    var = jnp.mean(center * center, -1, keepdims=True)
    inverse = lax.rsqrt(var + eps)
    normed = center * inverse
    return (normed * gain + shift, normed, inverse)


def norm_back(grad, normed, inverse, gain):
    scaled = grad * gain
    inner = (
        scaled
        - jnp.mean(scaled, -1, keepdims=True)
        - normed * jnp.mean(scaled * normed, -1, keepdims=True)
    )
    return inner * inverse


def turning(position):
    lane = jnp.arange(128, dtype=jnp.int32) % HD
    half = ROT // 2
    freq = 10000.0 ** (-(lane % half).astype(f32) / half)
    angle = position.astype(f32)[:, None] * jnp.where(lane < ROT, freq, 0.0)[None, :]
    return jnp.cos(angle), jnp.sin(angle) * jnp.where(lane < half, -1.0, 1.0)[None, :]


def turned(values, cosine, sine):
    wide = values.shape[1]
    half = ROT // 2
    lane = lax.broadcasted_iota(jnp.int32, values.shape, 1) & (HD - 1)
    partner = jnp.where(lane < half, pltpu.roll(values, wide - half, 1), pltpu.roll(values, half, 1))
    return values * cosine + partner * sine


def widened(table, wide):
    return table if wide == table.shape[1] else jnp.concatenate([table] * (wide // table.shape[1]), 1)


def head_lanes(shape, head):
    return lax.broadcasted_iota(jnp.int32, shape, len(shape) - 1) // HD == head


def dot(left, right, over):
    return lax.dot_general(left, right, (over, ((), ())), preferred_element_type=f32)


def forward_kernel(lens, mixed, shift, cosine, sine, column, line, qkv_ref, low_ref, full_ref, sums_ref):
    wide = mixed.shape[-1] // 3
    length = line.shape[1]
    values = mixed[...].reshape(length, 3 * wide) + shift[...]
    cos, sin = widened(cosine[...], wide), widened(sine[...], wide)
    query = (turned(values[:, :wide], cos, sin) * 0.125).astype(bf16)
    keys = turned(values[:, wide : 2 * wide], cos, sin).astype(bf16)
    vals = values[:, 2 * wide :].astype(bf16)
    for place, part in enumerate((query, keys, vals)):
        qkv_ref[:, :, :, place * wide : (place + 1) * wide] = part.reshape(qkv_ref.shape[:-1] + (wide,))
    size = min(512, length)
    blocks = mixed.shape[0] * size // length
    limit = lens[pl.program_id(0)]
    for start in range(0, length, size):
        rows = slice(start, start + size)
        valid = (line[...] <= column[rows]) & (line[...] < limit)
        out = jnp.zeros((size, wide), f32)
        kept = jnp.zeros((size, 128), f32)
        for head in range(wide // HD):
            here = head_lanes((size, wide), head)
            scores = dot(jnp.where(here, query[rows], 0), keys, ((1,), (1,)))
            scores = jnp.where(valid, scores, -1e30)
            top = jnp.max(scores, 1, keepdims=True)
            weights = jnp.exp(scores - top)
            total = jnp.sum(weights, 1, keepdims=True)
            probs = (weights * (1.0 / total)).astype(bf16)
            out = jnp.where(here, dot(probs, vals, ((1,), (0,))), out)
            lane = lax.broadcasted_iota(jnp.int32, kept.shape, 1)
            kept = jnp.where(lane == head, top + jnp.log(total), kept)
        at = slice(start // size * blocks, (start // size + 1) * blocks)
        low_ref[at] = out.astype(bf16).reshape((blocks,) + low_ref.shape[1:])
        full_ref[at] = out.reshape((blocks,) + full_ref.shape[1:])
        sums_ref[0, rows] = kept


def backward_kernel(lens, qkv, grad, full, sums, cosine, sine, column, line, out_ref, bias_ref):
    wide = grad.shape[-1]
    length = line.shape[1]
    values = qkv[...].reshape(length, 3 * wide)
    query, keys, vals = (values[:, i * wide : (i + 1) * wide] for i in range(3))
    grads = grad[...].reshape(length, wide)
    attended = full[...].reshape(length, wide)
    size = min(512, length)
    limit = lens[pl.program_id(0)]
    grad_query = []
    grad_key = jnp.zeros((length, wide), f32)
    grad_val = jnp.zeros((length, wide), f32)
    for start in range(0, length, size):
        rows = slice(start, start + size)
        valid = (line[...] <= column[rows]) & (line[...] < limit)
        both = grads[rows].astype(f32) * attended[rows]
        grad_here = jnp.zeros((size, wide), f32)
        for head in range(wide // HD):
            here = head_lanes((size, wide), head)
            own_query = jnp.where(here, query[rows], 0)
            own_grad = jnp.where(here, grads[rows], 0)
            own_keys = jnp.where(head_lanes((length, wide), head), keys, 0)
            delta = jnp.sum(jnp.where(here, both, 0.0), 1, keepdims=True)
            scores = dot(own_query, keys, ((1,), (1,)))
            probs = jnp.where(valid, jnp.exp(scores - sums[0, rows, head : head + 1]), 0.0)
            grad_val = grad_val + dot(probs.astype(bf16), own_grad, ((0,), (0,)))
            grad_prob = dot(own_grad, vals, ((1,), (1,)))
            grad_score = (probs * (grad_prob - delta)).astype(bf16)
            grad_here = grad_here + dot(grad_score, own_keys, ((1,), (0,)))
            grad_key = grad_key + dot(grad_score, own_query, ((0,), (0,)))
        grad_query.append(grad_here)
    cos, sin = widened(cosine[...], wide), -widened(sine[...], wide)
    grad_query = turned(joined(grad_query) * 0.125, cos, sin)
    grad_key = turned(grad_key, cos, sin)
    for place, part in enumerate((grad_query, grad_key, grad_val)):
        part = part.astype(bf16)
        at = slice(place * wide, (place + 1) * wide)
        out_ref[:, :, :, at] = part.reshape(out_ref.shape[:-1] + (wide,))
        bias_ref[0, :, at] = jnp.broadcast_to(jnp.sum(part.astype(f32), 0, keepdims=True), (8, wide))


def of_row(array):
    blocks, _, places, wide = array.shape
    return pl.BlockSpec((blocks, 1, places, wide), lambda r, lens: (0, r, 0, 0))


def entire(array):
    return pl.BlockSpec(array.shape, lambda r, lens: (0,) * array.ndim)


def attend_forward(mixed, shift, tables, lens):
    blocks, rows, places, wide = mixed.shape
    wide = wide // 3
    length = blocks * places
    out = [
        jax.ShapeDtypeStruct((blocks, rows, places, 3 * wide), bf16),
        jax.ShapeDtypeStruct((blocks, rows, places, wide), bf16),
        jax.ShapeDtypeStruct((blocks, rows, places, wide), f32),
        jax.ShapeDtypeStruct((rows, length, 128), f32),
    ]
    return pl.pallas_call(
        forward_kernel,
        out_shape=out,
        grid_spec=pltpu.PrefetchScalarGridSpec(
            num_scalar_prefetch=1,
            grid=(rows,),
            in_specs=[of_row(mixed), entire(shift)] + [entire(t) for t in tables],
            out_specs=[of_row(o) for o in out[:3]]
            + [pl.BlockSpec((1, length, 128), lambda r, lens: (r, 0, 0))],
        ),
        compiler_params=pltpu.CompilerParams(vmem_limit_bytes=40 << 20),
        name="attend_forward",
    )(lens, mixed, shift, *tables)


def attend_backward(qkv, grad, full, sums, tables, lens):
    blocks, rows, places, wide = grad.shape
    length = blocks * places
    out = [
        jax.ShapeDtypeStruct(qkv.shape, bf16),
        jax.ShapeDtypeStruct((rows, 8, 3 * wide), f32),
    ]
    return pl.pallas_call(
        backward_kernel,
        out_shape=out,
        grid_spec=pltpu.PrefetchScalarGridSpec(
            num_scalar_prefetch=1,
            grid=(rows,),
            in_specs=[
                of_row(qkv),
                of_row(grad),
                of_row(full),
                pl.BlockSpec((1, length, 128), lambda r, lens: (r, 0, 0)),
            ]
            + [entire(t) for t in tables],
            out_specs=[of_row(out[0]), pl.BlockSpec((1, 8, 3 * wide), lambda r, lens: (r, 0, 0))],
        ),
        compiler_params=pltpu.CompilerParams(vmem_limit_bytes=48 << 20),
        name="attend_backward",
    )(lens, qkv, grad, full, sums, *tables)


def body(
    inputs,
    cotangent,
    lengths,
    norm_params,
    entry_weight,
    entry_bias,
    output_weight,
    gate_weight,
    down_weight,
    moment_norm,
    moment_entry,
    moment_bias,
    moment_output,
    moment_gate,
    moment_down,
    average_norm,
    average_entry,
    average_bias,
    average_output,
    average_gate,
    average_down,
):
    plan = Plan(inputs.shape[1])
    gate_master, down_master = gate_weight, down_weight
    groups, parts, rows = plan.groups, plan.parts, plan.rows
    block_len, _, width = inputs.shape
    tp_width = entry_weight.shape[2]
    head_width = tp_width // parts
    heads_here = head_width // HD
    hidden = gate_weight.shape[2] // parts
    quarter = block_len // plan.n_tp
    share = rows * groups * quarter
    plan.total = share * plan.members
    length = block_len * plan.n_seq

    member_seq = np.array([plan.member_masks(k)[0] for k in range(plan.members)], np.int32)
    member_tp = np.array([plan.member_masks(k)[1] for k in range(plan.members)], np.int32)
    sender = np.array([plan.outer_mask(j) for j in range(groups)], np.int32)
    seq_at = plan.seq ^ (member_seq[:, None] | sender[None, :])
    tp_at = plan.tp ^ member_tp
    position = (
        (seq_at * block_len)[:, :, None]
        + (tp_at * quarter)[:, None, None]
        + np.arange(quarter, dtype=np.int32)[None, None, :]
    )
    lens = lax.dynamic_slice_in_dim(lengths, plan.group * rows, rows, 0)

    def over_masks(array, masks):
        sums = [0]
        for mask in masks:
            sums = sums + [m | mask for m in sums]
        return [swap(array, "seq", m) for m in sums[1:]]

    def total_of(array, got):
        for other in got:
            array = array + other
        return array

    lane_block = lax.broadcasted_iota(jnp.int32, (4, width), 1) // norm_params.shape[1]
    small = jnp.where(lane_block == plan.seq, jnp.tile(norm_params.astype(bf16), (1, plan.n_seq)), 0)
    slim = entry_bias.shape[2]
    slot = lax.broadcasted_iota(jnp.int32, (slim, HD), 1) == plan.seq * slim + lax.broadcasted_iota(
        jnp.int32, (slim, HD), 0
    )
    placed = jnp.dot(entry_bias.reshape(-1, slim).astype(bf16), slot.astype(bf16), preferred_element_type=f32)
    placed = placed.astype(bf16).reshape(1, 3 * tp_width)
    placed = jnp.pad(placed, ((0, 0), (0, width - 3 * tp_width)))
    small = jnp.concatenate([small, placed], 0)
    seq_masks = [1 << i for i in range(plan.n_seq.bit_length() - 1)]
    last_mask = plan.outer[-1]
    first_masks = [m for m in seq_masks if m != last_mask]

    def columns(array, h, size):
        return array[..., h * size : (h + 1) * size].astype(bf16).reshape(array.shape[0], -1)

    def turned_columns(array, h):
        return array[:, h * hidden : (h + 1) * hidden].astype(bf16).T

    attn_mine = pick(
        [
            jnp.concatenate(
                [columns(entry_weight, h, head_width), columns(output_weight, h, head_width)], 1
            )
            for h in range(parts)
        ],
        plan.part_flags,
    )
    attn_block = plan.spread_mine(attn_mine, 0)
    resid = plan.over_groups(plan.outgoing_rows(inputs))
    attn_block, resid, small, gate_weight, down_weight, cotangent, position = hold(
        attn_block, resid, small, gate_weight, down_weight, cotangent, position
    )

    w_attn = plan.all_blocks(attn_block)
    small_got = over_masks(small, first_masks)
    gate_mine = pick([columns(gate_weight, h, hidden) for h in range(parts)], plan.part_flags)
    gate_block = plan.spread_mine(gate_mine, 0)
    small, small_got, resid, gate_block, cotangent, down_weight, position = hold(
        small, small_got, resid, gate_block, cotangent, down_weight, position
    )

    small = total_of(small, small_got)
    small_got = over_masks(small, [last_mask])
    down_mine = pick([columns(down_weight, h, hidden) for h in range(parts)], plan.part_flags)
    down_block = plan.spread_mine(down_mine, 0)
    small, small_got, down_block, gate_block, cotangent = hold(
        small, small_got, down_block, gate_block, cotangent
    )

    small = total_of(small, small_got)
    gains = plan.arranged(small[:4]).astype(f32)
    resid = plan.arranged(jnp.concatenate(resid, 0)).astype(f32)
    h_first, n_first, i_first = layer_norm(resid, gains[0], gains[1])
    low_first = h_first.astype(bf16)
    sides = plan.chips_sides(low_first)
    row_position = position.reshape(length)
    tables = turning(row_position) + (row_position[:, None], row_position[None, :])
    blank = jnp.zeros((down_block.shape[0], -(2 * hidden + hidden) % 128), bf16)
    ffn_block = jnp.concatenate([gate_block, down_block, blank], 1)
    low_first, sides, tables, ffn_block, cotangent = hold(low_first, sides, tables, ffn_block, cotangent)
    corner = plan.chips_corner(low_first, sides)
    outgoing = plan.outgoing_rows(cotangent)
    low_first, sides, corner, outgoing = hold(low_first, sides, corner, outgoing)
    near = plan.chips_near(low_first, sides, corner)
    other = plan.swap_core(near)
    a_first = jnp.concatenate([near, other], 0)
    a_first, w_attn, ffn_block, outgoing = hold(a_first, w_attn, ffn_block, outgoing)
    w_ffn = plan.all_blocks(ffn_block)
    grad_y = plan.over_groups(outgoing)
    own_position = jnp.broadcast_to(position[0][:, None, :], (groups, rows, quarter))
    real = (own_position < lens[None, :, None]).reshape(share, 1)

    w_entry = w_attn[:, : 3 * head_width]
    w_output = w_attn[:, 3 * head_width :]
    mixed = jnp.einsum("td,df->tf", a_first, w_entry, preferred_element_type=f32)
    mixed = mixed.reshape(plan.members * groups, rows, quarter, 3 * head_width)
    biases = [
        jnp.concatenate(
            [
                small[4:, c * tp_width + h * head_width : c * tp_width + (h + 1) * head_width]
                for c in range(3)
            ],
            1,
        )
        for h in range(parts)
    ]
    entry_shift = pick(biases, plan.part_flags)[0].astype(f32)
    qkv, att_low, attended, score_sums = attend_forward(mixed, entry_shift, tables, lens)
    att_low = att_low.reshape(plan.total, head_width)

    def output_product(lo, hi):
        return jnp.einsum("th,dh->td", att_low[lo:hi], w_output, preferred_element_type=f32)

    half = plan.total // 2
    far_product = output_product(half, plan.total).astype(bf16)
    far_product, grad_y = hold(far_product, grad_y)

    got = plan.swap_core(far_product)
    product = output_product(0, half)
    grad_y = plan.arranged(jnp.concatenate(grad_y, 0))
    grad_y = jnp.where(real, grad_y, 0)
    product, got, grad_y = hold(product, got, grad_y)

    near = (product, got)
    corner = plan.sum_corner(near)
    y_sides = plan.chips_sides(grad_y)
    near, corner, y_sides = hold(near, corner, y_sides)
    sides = plan.sum_sides(near, corner)
    y_corner = plan.chips_corner(grad_y, y_sides)
    near, sides, y_corner = hold(near, sides, y_corner)

    second = resid + plan.sum_end(near, sides)
    h_second, n_second, i_second = layer_norm(second, gains[2], gains[3])
    low_second = h_second.astype(bf16)
    sides = plan.chips_sides(low_second)
    y_near = plan.chips_near(grad_y, y_sides, y_corner)
    y_other = plan.swap_core(y_near)
    second, low_second, sides, y_near, y_other = hold(second, low_second, sides, y_near, y_other)
    corner = plan.chips_corner(low_second, sides)
    grad_y_all = jnp.concatenate([y_near, y_other], 0)
    low_second, sides, corner, grad_y_all = hold(low_second, sides, corner, grad_y_all)
    near = plan.chips_near(low_second, sides, corner)
    other = plan.swap_core(near)
    a_second = jnp.concatenate([near, other], 0)
    a_second, w_ffn = hold(a_second, w_ffn)

    w_gate = w_ffn[:, : 2 * hidden]
    gated = jnp.einsum("td,df->tf", a_second, w_gate, preferred_element_type=f32)
    gate = gated[:, :hidden]
    upper = gated[:, hidden:]
    sigma = jax.nn.sigmoid(gate)
    active_gate = gate * sigma
    hid = (active_gate * upper).astype(bf16)
    grad_down = jnp.einsum("td,tf->df", grad_y_all, hid, preferred_element_type=f32).astype(bf16)
    hid, grad_down, w_ffn = hold(hid, grad_down, w_ffn)
    w_down = w_ffn[:, 2 * hidden : 3 * hidden]
    down_sum = plan.sum_blocks(grad_down)
    grad_hidden = jnp.einsum(
        "td,df->tf", grad_y_all, w_down, preferred_element_type=f32
    ).astype(bf16)
    grad_gate_val = grad_hidden * upper * (sigma * (1.0 + gate * (1.0 - sigma)))
    grad_up_val = grad_hidden * active_gate
    grad_gated = jnp.concatenate([grad_gate_val, grad_up_val], 1).astype(bf16)

    def gate_product(lo, hi):
        return jnp.einsum("tf,df->td", grad_gated[lo:hi], w_gate, preferred_element_type=f32)

    def down_product(lo, hi):
        return jnp.einsum("tf,df->td", hid[lo:hi], w_down, preferred_element_type=f32)

    far_product = gate_product(half, plan.total).astype(bf16)
    hid, grad_gated, far_product = hold(hid, grad_gated, far_product)

    got = plan.swap_core(far_product)
    product = gate_product(0, half)
    grad_gate = jnp.einsum("td,tf->df", a_second, grad_gated, preferred_element_type=f32).astype(bf16)
    product, got, hid, grad_gate, down_sum = hold(product, got, hid, grad_gate, down_sum)
    gate_sum = plan.sum_blocks(grad_gate)

    near = (product, got)
    corner = plan.sum_corner(near)
    near, corner, hid, down_sum = hold(near, corner, hid, down_sum)
    sides = plan.sum_sides(near, corner)
    out_far = down_product(half, plan.total).astype(bf16)
    near, sides, out_far, hid, down_sum = hold(near, sides, out_far, hid, down_sum)

    out_got = plan.swap_core(out_far)
    grad_h2 = plan.sum_end(near, sides)
    grad_second = grad_y.astype(f32) + norm_back(grad_h2, n_second, i_second, gains[2])
    low_grad = grad_second.astype(bf16)
    sides = plan.chips_sides(low_grad)
    out_near = down_product(0, half)
    low_grad, sides, out_near, out_got, grad_h2, grad_second = hold(
        low_grad, sides, out_near, out_got, grad_h2, grad_second
    )
    out_near = (out_near, out_got)
    corner = plan.chips_corner(low_grad, sides)
    out_corner = plan.sum_corner(out_near)
    low_grad, sides, corner, out_corner, out_near = hold(low_grad, sides, corner, out_corner, out_near)

    near = plan.chips_near(low_grad, sides, corner)
    other = plan.swap_core(near)
    near, other = hold(near, other)
    grad_second_all = jnp.concatenate([near, other], 0)
    grad_att = jnp.einsum(
        "td,dh->th", grad_second_all, w_output, preferred_element_type=f32
    ).astype(bf16)
    grad_att = grad_att.reshape(attended.shape)
    grad_mixed, bias_sum = attend_backward(qkv, grad_att, attended, score_sums, tables, lens)
    grad_mixed = grad_mixed.reshape(plan.total, 3 * head_width)

    def entry_product(lo, hi):
        return jnp.einsum("tf,df->td", grad_mixed[lo:hi], w_entry, preferred_element_type=f32)

    far_product = entry_product(half, plan.total).astype(bf16)
    out_sides = plan.sum_sides(out_near, out_corner)
    far_product, grad_mixed, bias_sum, out_sides, out_near = hold(
        far_product, grad_mixed, bias_sum, out_sides, out_near
    )

    got = plan.swap_core(far_product)
    product = entry_product(0, half)
    grad_attn = jnp.concatenate(
        [
            jnp.einsum("td,tf->df", a_first, grad_mixed, preferred_element_type=f32).astype(bf16),
            jnp.einsum("td,tf->df", grad_second_all, att_low, preferred_element_type=f32).astype(bf16),
        ],
        1,
    )
    bias_sum = jnp.sum(bias_sum[:, 0], 0, keepdims=True)
    bias_got = over_masks(bias_sum, plan.outer)
    result = second + plan.sum_end(out_near, out_sides)
    out_back = plan.over_groups(plan.returning_rows(result.astype(bf16)))
    product, got, grad_attn, bias_sum, bias_got, down_sum, out_back, gate_sum = hold(
        product, got, grad_attn, bias_sum, bias_got, down_sum, out_back, gate_sum
    )
    attn_sum = plan.sum_blocks(grad_attn)

    bias_sum = total_of(bias_sum, bias_got)
    near = (product, got)
    corner = plan.sum_corner(near)
    bias_got = [swap(bias_sum, "seq", plan.inner_mask(j)) for j in range(1, parts)]
    near, corner, bias_sum, bias_got, down_sum, gate_sum, out_back = hold(
        near, corner, bias_sum, bias_got, down_sum, gate_sum, out_back
    )
    sides = plan.sum_sides(near, corner)
    near, sides, out_back, down_sum, gate_sum = hold(near, sides, out_back, down_sum, gate_sum)

    def along_tp(own):
        return gather(own, [("tp", m, m) for m in plan.tp_masks[:0:-1]])

    grad_h1 = plan.sum_end(near, sides)
    grad_input = grad_second + norm_back(grad_h1, n_first, i_first, gains[0])
    back = plan.over_groups(plan.returning_rows(grad_input.astype(bf16)))
    grad_gate = plan.collect_home(gate_sum)
    grad_down = plan.collect_home(down_sum)
    out_pieces = along_tp(plan.returned_rows(out_back, quarter, inputs.shape[1]))
    sums = jnp.stack(
        [
            jnp.sum(grad_h1 * n_first, 0),
            jnp.sum(grad_h1, 0),
            jnp.sum(grad_h2 * n_second, 0),
            jnp.sum(grad_h2, 0),
        ]
    )
    for mask in plan.tp_masks:
        sums = sums + swap(sums, "tp", mask)
    sums = plan.restored(sums)
    for mask in seq_masks:
        sums = sums + swap(sums, "seq", mask)
    back, grad_gate, grad_down, out_pieces, sums, attn_sum = hold(
        back, grad_gate, grad_down, out_pieces, sums, attn_sum
    )

    def ordered_as(grad, *order):
        return with_layout_constraint(grad, Layout(order))

    beta = min(0.999, (1 + STEP) / (10 + STEP))

    def stepped(index, grad, master, moment, average):
        grad = grad + decays[index] * master
        moment = 0.9 * moment + grad
        weight = master - rates[index] * (grad + 0.9 * moment)
        return moment, weight, beta * average + (1.0 - beta) * weight, weight.astype(bf16)

    grad_gate = ordered_as(
        joined([part.reshape(part.shape[0], 2, hidden) for part in grad_gate], -1), 0, 1, 2
    )
    gate = stepped(4, grad_gate, gate_master, moment_gate, average_gate)
    grad_down = ordered_as(joined(grad_down, -1), 0, 1)
    down = stepped(5, grad_down, down_master, moment_down, average_down)
    core_masks = plan.tp_masks[:1]
    pieces = along_tp(plan.returned_rows(back, quarter, inputs.shape[1]))
    attn_home = plan.collect_home(attn_sum)

    def across_cores(pieces):
        keys = sorted(pieces)
        got = swap(joined([pieces[k] for k in keys]), "tp", core_masks[0])
        size = got.shape[0] // len(keys)
        pieces = {**pieces, **{k | core_masks[0]: got[i * size : (i + 1) * size] for i, k in enumerate(keys)}}
        return plan.of_tp(pieces).reshape(inputs.shape)

    layer_out = across_cores(out_pieces)
    pieces, sums, layer_out, gate, down, attn_home = hold(pieces, sums, layer_out, gate, down, attn_home)

    input_grad = across_cores(pieces)

    got = [part.reshape(3, heads_here, HD) for part in [bias_sum] + bias_got]
    bias_sum = joined(pick(got, plan.part_flags), 1)
    grad_bias = lax.dynamic_slice_in_dim(bias_sum, plan.seq * slim, slim, 2)
    slim = norm_params.shape[1]
    grad_norm = lax.dynamic_slice_in_dim(sums, plan.seq * slim, slim, 1)

    norm = stepped(0, grad_norm, norm_params, moment_norm, average_norm)
    bias = stepped(2, grad_bias, entry_bias, moment_bias, average_bias)

    def turned_over(array):
        return jnp.swapaxes(array, 0, 1)

    grad_entry = jnp.stack(
        [
            joined([part[:, c * head_width : (c + 1) * head_width] for part in attn_home], -1)
            for c in range(3)
        ]
    )
    grad_output = ordered_as(joined([part[:, 3 * head_width :] for part in attn_home], -1), 0, 1)
    entry = stepped(
        1, grad_entry, turned_over(entry_weight), turned_over(moment_entry), turned_over(average_entry)
    )
    entry = [turned_over(array) for array in entry]
    output = stepped(3, grad_output, output_weight, moment_output, average_output)
    kinds = zip(norm, entry, bias, output, gate, down)
    return (layer_out, input_grad, *(array for kind in kinds for array in kind))


def solution(mesh):
    in_specs = (
        P("seq", None, None),
        P("seq", None, None),
        P(),
        P(None, "seq"),
        P("seq", None, "tp"),
        P(None, "tp", "seq"),
        P("seq", "tp"),
        P("seq", None, "tp"),
        P("seq", "tp"),
        P(None, "seq"),
        P("seq", None, "tp"),
        P(None, "tp", "seq"),
        P("seq", "tp"),
        P("seq", None, "tp"),
        P("seq", "tp"),
        P(None, "seq"),
        P("seq", None, "tp"),
        P(None, "tp", "seq"),
        P("seq", "tp"),
        P("seq", None, "tp"),
        P("seq", "tp"),
    )
    out_specs = (
        P("seq", None, None),
        P("seq", None, None),
        P(None, "seq"),
        P("seq", None, "tp"),
        P(None, "tp", "seq"),
        P("seq", "tp"),
        P("seq", None, "tp"),
        P("seq", "tp"),
        P(None, "seq"),
        P("seq", None, "tp"),
        P(None, "tp", "seq"),
        P("seq", "tp"),
        P("seq", None, "tp"),
        P("seq", "tp"),
        P(None, "seq"),
        P("seq", None, "tp"),
        P(None, "tp", "seq"),
        P("seq", "tp"),
        P("seq", None, "tp"),
        P("seq", "tp"),
        P(None, "seq"),
        P("seq", None, "tp"),
        P(None, "tp", "seq"),
        P("seq", "tp"),
        P("seq", None, "tp"),
        P("seq", "tp"),
    )
    return jax.shard_map(body, mesh=mesh, in_specs=in_specs, out_specs=out_specs, check_vma=False)
```

```python
import numpy as np

import jax
import jax.numpy as jnp
from jax import lax
from jax.experimental import pallas as pl
from jax.experimental.layout import Layout, with_layout_constraint
from jax.experimental.pallas import tpu as pltpu
from jax.sharding import PartitionSpec as P

HD = 64
ROT = 16
STEP = 10

eps = 1e-05
rates = (0.0005, 0.0002, 0.0025, 0.004, 0.0002, 6e-05)
decays = (0.0, 0.0001, 0.0, 0.0001, 0.0001, 0.0001)
bf16 = jnp.bfloat16
f32 = jnp.float32


def swap(array, axis, mask):
    pairs = [(i, i ^ mask) for i in range(lax.axis_size(axis))]
    return lax.ppermute(array, axis, pairs)


def pick(parts, flags):
    count = len(parts)
    for place, flag in enumerate(flags):
        bit = count >> (place + 1)
        parts = [jnp.where(flag, parts[j ^ bit], parts[j]) for j in range(count)]
    return parts


def joined(parts, axis=0):
    return parts[0] if len(parts) == 1 else jnp.concatenate(parts, axis)


def gather(piece, steps):
    pieces = {0: piece}
    rows = piece.shape[0]
    for axis, mask, bit in steps:
        keys = sorted(pieces)
        got = swap(joined([pieces[k] for k in keys]), axis, mask)
        for place, k in enumerate(keys):
            pieces[k | bit] = got[place * rows : (place + 1) * rows]
    return pieces


def scatter(pieces, steps):
    for axis, mask, bit in steps:
        keys = sorted(k for k in pieces if k & bit)
        got = swap(joined([pieces[k].astype(bf16) for k in keys]), axis, mask)
        rows = got.shape[0] // len(keys)
        kept = {k: v for k, v in pieces.items() if not k & bit}
        for place, k in enumerate(keys):
            kept[k ^ bit] = kept[k ^ bit].astype(f32) + got[place * rows : (place + 1) * rows].astype(f32)
        pieces = kept
    return pieces[0]


def added(near, start, stop):
    return near[0][start:stop] + near[1][start:stop].astype(f32)


class Plan:
    def __init__(self, rows):
        self.n_seq = lax.axis_size("seq")
        self.n_tp = lax.axis_size("tp")
        self.seq = lax.axis_index("seq")
        self.tp = lax.axis_index("tp")
        bits = self.n_seq.bit_length() - 1
        self.inner = [1 << i for i in range(bits // 2)][::-1]
        self.outer = [1 << i for i in range(bits) if (1 << i) not in self.inner][::-1]
        self.groups = 1 << len(self.outer)
        self.parts = 1 << len(self.inner)
        self.rows = rows // self.groups
        self.group_flags = [(self.seq & m) != 0 for m in self.outer]
        self.part_flags = [(self.seq & m) != 0 for m in self.inner]
        self.tp_masks = [1 << i for i in range(self.n_tp.bit_length() - 1)]
        self.tp_flags = [(self.tp & m) != 0 for m in self.tp_masks[::-1]]
        self.group = self.index(self.group_flags)
        order = [("tp", m) for m in self.tp_masks] + [("seq", m) for m in self.inner]
        self.members = 1 << len(order)
        self.steps = [(axis, mask, self.members >> (i + 1)) for i, (axis, mask) in enumerate(order)]
        self.group_steps = [("seq", m, self.groups >> (i + 1)) for i, m in enumerate(self.outer)]

    def index(self, flags):
        value = jnp.int32(0)
        for flag in flags:
            value = value * 2 + flag.astype(jnp.int32)
        return value

    def outer_mask(self, j):
        return sum(m for i, m in enumerate(self.outer) if j & (self.groups >> (i + 1)))

    def inner_mask(self, j):
        return sum(m for i, m in enumerate(self.inner) if j & (self.parts >> (i + 1)))

    def member_masks(self, k):
        seq = sum(m for a, m, bit in self.steps if a == "seq" and k & bit)
        tp = sum(m for a, m, bit in self.steps if a == "tp" and k & bit)
        return seq, tp

    def arranged(self, array):
        wide = array.shape[-1] // self.n_seq
        places = [self.outer_mask(g) | self.inner_mask(h) for g in range(self.groups) for h in range(self.parts)]
        return joined([array[..., p * wide : (p + 1) * wide] for p in places], -1)

    def restored(self, array):
        wide = array.shape[-1] // self.n_seq
        blocks = [None] * self.n_seq
        for g in range(self.groups):
            for h in range(self.parts):
                at = g * self.parts + h
                blocks[self.outer_mask(g) | self.inner_mask(h)] = array[..., at * wide : (at + 1) * wide]
        return joined(blocks, -1)

    def lists(self):
        return [
            [self.outer_mask(g) | self.inner_mask(h) for g in range(self.groups)] for h in range(self.parts)
        ]

    def chosen(self, j, part, all_rows):
        row = lax.broadcasted_iota(jnp.int32, (self.rows * part, part * all_rows), 0)
        column = lax.broadcasted_iota(jnp.int32, (self.rows * part, part * all_rows), 1)
        source = (row % part) * all_rows + (self.group ^ j) * self.rows + row // part
        return (column == source).astype(bf16)

    def outgoing_rows(self, array):
        block, all_rows, width = array.shape
        part = block // self.n_tp
        size = part * all_rows
        own = lax.dynamic_slice_in_dim(array.reshape(-1, width), self.tp * size, size, 0)
        return [
            jnp.dot(self.chosen(j, part, all_rows), own, preferred_element_type=f32).astype(bf16)
            for j in range(self.groups)
        ]

    def over_groups(self, pieces):
        return [swap(piece, "seq", self.outer_mask(j)) if j else piece for j, piece in enumerate(pieces)]

    def returning_rows(self, tokens):
        table = self.restored(tokens)
        size = table.shape[0] // self.groups
        return [table[j * size : (j + 1) * size] for j in range(self.groups)]

    def returned_rows(self, got, part, all_rows):
        back = jnp.concatenate([self.chosen(j, part, all_rows) for j in range(self.groups)], 0)
        return jnp.einsum("sp,sd->pd", back, jnp.concatenate(got, 0), preferred_element_type=f32).astype(bf16)

    def of_tp(self, pieces):
        return joined(pick([pieces[k] for k in range(self.n_tp)], self.tp_flags), 0)

    def chips_sides(self, piece):
        far = self.steps[1:]
        if len(far) != 2:
            return gather(piece, far)
        return [swap(piece, axis, mask) for axis, mask, _ in far]

    def chips_corner(self, piece, sides):
        far = self.steps[1:]
        if len(far) != 2:
            return sides
        half = piece.shape[0] // 2
        (axis_x, mask_x, _), (axis_z, mask_z, _) = far
        return [swap(sides[0][:half], axis_z, mask_z), swap(sides[1][half:], axis_x, mask_x)]

    def chips_near(self, piece, sides, corner):
        if len(self.steps) != 3:
            return joined([sides[k] for k in sorted(sides)])
        return jnp.concatenate([piece, sides[1], sides[0], corner[0], corner[1]], 0)

    def swap_core(self, array):
        axis, mask, _ = self.steps[0]
        return swap(array, axis, mask)

    def sum_corner(self, near):
        far = self.steps[1:]
        rows = near[0].shape[0] >> len(far)
        if len(far) != 2:
            return [scatter({k: added(near, k * rows, (k + 1) * rows) for k in range(1 << len(far))}, far)]
        (axis_x, mask_x, _), (axis_z, mask_z, _) = far
        middle = 3 * rows + rows // 2
        one = added(near, 3 * rows, middle).astype(bf16)
        two = added(near, middle, 4 * rows).astype(bf16)
        return [swap(one, axis_x, mask_x), swap(two, axis_z, mask_z)]

    def sum_sides(self, near, corner):
        far = self.steps[1:]
        if len(far) != 2:
            return corner
        (axis_x, mask_x, _), (axis_z, mask_z, _) = far
        rows = near[0].shape[0] // 4
        half = rows // 2
        one, two = added(near, rows, 2 * rows), added(near, 2 * rows, 3 * rows)
        for_z = jnp.concatenate([one[:half] + corner[0].astype(f32), one[half:]], 0).astype(bf16)
        for_x = jnp.concatenate([two[:half], two[half:] + corner[1].astype(f32)], 0).astype(bf16)
        return [swap(for_z, axis_z, mask_z), swap(for_x, axis_x, mask_x)]

    def sum_end(self, near, sides):
        if len(self.steps) != 3:
            return sides[0]
        rows = near[0].shape[0] // 4
        return added(near, 0, rows) + sides[0].astype(f32) + sides[1].astype(f32)

    def spread_mine(self, mine, axis):
        got = [mine[0]] + [swap(mine[j], "seq", self.inner_mask(j)) for j in range(1, self.parts)]
        return joined(pick(got, self.part_flags), axis)

    def collect_home(self, block_sum):
        rows = block_sum.shape[0] // self.parts
        blocks = [block_sum[h * rows : (h + 1) * rows] for h in range(self.parts)]
        mine = pick(blocks, self.part_flags)
        got = [mine[0].astype(f32)] + [
            swap(mine[j].astype(bf16), "seq", self.inner_mask(j)).astype(f32) for j in range(1, self.parts)
        ]
        return pick(got, self.part_flags)

    def all_blocks(self, block):
        return lax.all_gather(block, "seq", axis_index_groups=self.lists(), axis=0, tiled=True)

    def sum_blocks(self, product):
        return lax.psum_scatter(
            product, "seq", scatter_dimension=0, axis_index_groups=self.lists(), tiled=True
        )


def hold(*values):
    return lax.optimization_barrier(values)


def layer_norm(values, gain, shift):
    center = values - jnp.mean(values, -1, keepdims=True)
    var = jnp.mean(center * center, -1, keepdims=True)
    inverse = lax.rsqrt(var + eps)
    normed = center * inverse
    return (normed * gain + shift, normed, inverse)


def norm_back(grad, normed, inverse, gain):
    scaled = grad * gain
    inner = (
        scaled
        - jnp.mean(scaled, -1, keepdims=True)
        - normed * jnp.mean(scaled * normed, -1, keepdims=True)
    )
    return inner * inverse


def turning(position):
    lane = jnp.arange(128, dtype=jnp.int32) % HD
    half = ROT // 2
    freq = 10000.0 ** (-(lane % half).astype(f32) / half)
    angle = position.astype(f32)[:, None] * jnp.where(lane < ROT, freq, 0.0)[None, :]
    return jnp.cos(angle), jnp.sin(angle) * jnp.where(lane < half, -1.0, 1.0)[None, :]


def turned(values, cosine, sine):
    wide = values.shape[1]
    half = ROT // 2
    lane = lax.broadcasted_iota(jnp.int32, values.shape, 1) & (HD - 1)
    partner = jnp.where(lane < half, pltpu.roll(values, wide - half, 1), pltpu.roll(values, half, 1))
    return values * cosine + partner * sine


def widened(table, wide):
    return table if wide == table.shape[1] else jnp.concatenate([table] * (wide // table.shape[1]), 1)


def head_lanes(shape, head):
    return lax.broadcasted_iota(jnp.int32, shape, len(shape) - 1) // HD == head


def dot(left, right, over):
    return lax.dot_general(left, right, (over, ((), ())), preferred_element_type=f32)


def forward_kernel(lens, mixed, shift, cosine, sine, column, line, qkv_ref, low_ref, full_ref, sums_ref):
    wide = mixed.shape[-1] // 3
    length = line.shape[1]
    values = mixed[...].reshape(length, 3 * wide) + shift[...]
    cos, sin = widened(cosine[...], wide), widened(sine[...], wide)
    query = (turned(values[:, :wide], cos, sin) * 0.125).astype(bf16)
    keys = turned(values[:, wide : 2 * wide], cos, sin).astype(bf16)
    vals = values[:, 2 * wide :].astype(bf16)
    for place, part in enumerate((query, keys, vals)):
        qkv_ref[:, :, :, place * wide : (place + 1) * wide] = part.reshape(qkv_ref.shape[:-1] + (wide,))
    size = min(512, length)
    blocks = mixed.shape[0] * size // length
    limit = lens[pl.program_id(0)]
    for start in range(0, length, size):
        rows = slice(start, start + size)
        valid = (line[...] <= column[rows]) & (line[...] < limit)
        out = jnp.zeros((size, wide), f32)
        kept = jnp.zeros((size, 128), f32)
        for head in range(wide // HD):
            here = head_lanes((size, wide), head)
            scores = dot(jnp.where(here, query[rows], 0), keys, ((1,), (1,)))
            scores = jnp.where(valid, scores, -1e30)
            top = jnp.max(scores, 1, keepdims=True)
            weights = jnp.exp(scores - top)
            total = jnp.sum(weights, 1, keepdims=True)
            probs = (weights * (1.0 / total)).astype(bf16)
            out = jnp.where(here, dot(probs, vals, ((1,), (0,))), out)
            lane = lax.broadcasted_iota(jnp.int32, kept.shape, 1)
            kept = jnp.where(lane == head, top + jnp.log(total), kept)
        at = slice(start // size * blocks, (start // size + 1) * blocks)
        low_ref[at] = out.astype(bf16).reshape((blocks,) + low_ref.shape[1:])
        full_ref[at] = out.reshape((blocks,) + full_ref.shape[1:])
        sums_ref[0, rows] = kept


def backward_kernel(lens, qkv, grad, full, sums, cosine, sine, column, line, out_ref, bias_ref):
    wide = grad.shape[-1]
    length = line.shape[1]
    values = qkv[...].reshape(length, 3 * wide)
    query, keys, vals = (values[:, i * wide : (i + 1) * wide] for i in range(3))
    grads = grad[...].reshape(length, wide)
    attended = full[...].reshape(length, wide)
    size = min(512, length)
    limit = lens[pl.program_id(0)]
    grad_query = []
    grad_key = jnp.zeros((length, wide), f32)
    grad_val = jnp.zeros((length, wide), f32)
    for start in range(0, length, size):
        rows = slice(start, start + size)
        valid = (line[...] <= column[rows]) & (line[...] < limit)
        both = grads[rows].astype(f32) * attended[rows]
        grad_here = jnp.zeros((size, wide), f32)
        for head in range(wide // HD):
            here = head_lanes((size, wide), head)
            own_query = jnp.where(here, query[rows], 0)
            own_grad = jnp.where(here, grads[rows], 0)
            own_keys = jnp.where(head_lanes((length, wide), head), keys, 0)
            delta = jnp.sum(jnp.where(here, both, 0.0), 1, keepdims=True)
            scores = dot(own_query, keys, ((1,), (1,)))
            probs = jnp.where(valid, jnp.exp(scores - sums[0, rows, head : head + 1]), 0.0)
            grad_val = grad_val + dot(probs.astype(bf16), own_grad, ((0,), (0,)))
            grad_prob = dot(own_grad, vals, ((1,), (1,)))
            grad_score = (probs * (grad_prob - delta)).astype(bf16)
            grad_here = grad_here + dot(grad_score, own_keys, ((1,), (0,)))
            grad_key = grad_key + dot(grad_score, own_query, ((0,), (0,)))
        grad_query.append(grad_here)
    cos, sin = widened(cosine[...], wide), -widened(sine[...], wide)
    grad_query = turned(joined(grad_query) * 0.125, cos, sin)
    grad_key = turned(grad_key, cos, sin)
    for place, part in enumerate((grad_query, grad_key, grad_val)):
        part = part.astype(bf16)
        at = slice(place * wide, (place + 1) * wide)
        out_ref[:, :, :, at] = part.reshape(out_ref.shape[:-1] + (wide,))
        bias_ref[0, :, at] = jnp.broadcast_to(jnp.sum(part.astype(f32), 0, keepdims=True), (8, wide))


def of_row(array):
    blocks, _, places, wide = array.shape
    return pl.BlockSpec((blocks, 1, places, wide), lambda r, lens: (0, r, 0, 0))


def entire(array):
    return pl.BlockSpec(array.shape, lambda r, lens: (0,) * array.ndim)


def attend_forward(mixed, shift, tables, lens):
    blocks, rows, places, wide = mixed.shape
    wide = wide // 3
    length = blocks * places
    out = [
        jax.ShapeDtypeStruct((blocks, rows, places, 3 * wide), bf16),
        jax.ShapeDtypeStruct((blocks, rows, places, wide), bf16),
        jax.ShapeDtypeStruct((blocks, rows, places, wide), f32),
        jax.ShapeDtypeStruct((rows, length, 128), f32),
    ]
    return pl.pallas_call(
        forward_kernel,
        out_shape=out,
        grid_spec=pltpu.PrefetchScalarGridSpec(
            num_scalar_prefetch=1,
            grid=(rows,),
            in_specs=[of_row(mixed), entire(shift)] + [entire(t) for t in tables],
            out_specs=[of_row(o) for o in out[:3]]
            + [pl.BlockSpec((1, length, 128), lambda r, lens: (r, 0, 0))],
        ),
        compiler_params=pltpu.CompilerParams(vmem_limit_bytes=40 << 20),
        name="attend_forward",
    )(lens, mixed, shift, *tables)


def attend_backward(qkv, grad, full, sums, tables, lens):
    blocks, rows, places, wide = grad.shape
    length = blocks * places
    out = [
        jax.ShapeDtypeStruct(qkv.shape, bf16),
        jax.ShapeDtypeStruct((rows, 8, 3 * wide), f32),
    ]
    return pl.pallas_call(
        backward_kernel,
        out_shape=out,
        grid_spec=pltpu.PrefetchScalarGridSpec(
            num_scalar_prefetch=1,
            grid=(rows,),
            in_specs=[
                of_row(qkv),
                of_row(grad),
                of_row(full),
                pl.BlockSpec((1, length, 128), lambda r, lens: (r, 0, 0)),
            ]
            + [entire(t) for t in tables],
            out_specs=[of_row(out[0]), pl.BlockSpec((1, 8, 3 * wide), lambda r, lens: (r, 0, 0))],
        ),
        compiler_params=pltpu.CompilerParams(vmem_limit_bytes=48 << 20),
        name="attend_backward",
    )(lens, qkv, grad, full, sums, *tables)


def body(
    inputs,
    cotangent,
    lengths,
    norm_params,
    entry_weight,
    entry_bias,
    output_weight,
    gate_weight,
    down_weight,
    moment_norm,
    moment_entry,
    moment_bias,
    moment_output,
    moment_gate,
    moment_down,
    average_norm,
    average_entry,
    average_bias,
    average_output,
    average_gate,
    average_down,
):
    plan = Plan(inputs.shape[1])
    gate_master, down_master = gate_weight, down_weight
    groups, parts, rows = plan.groups, plan.parts, plan.rows
    block_len, _, width = inputs.shape
    tp_width = entry_weight.shape[2]
    head_width = tp_width // parts
    heads_here = head_width // HD
    hidden = gate_weight.shape[2] // parts
    quarter = block_len // plan.n_tp
    share = rows * groups * quarter
    plan.total = share * plan.members
    length = block_len * plan.n_seq

    member_seq = np.array([plan.member_masks(k)[0] for k in range(plan.members)], np.int32)
    member_tp = np.array([plan.member_masks(k)[1] for k in range(plan.members)], np.int32)
    sender = np.array([plan.outer_mask(j) for j in range(groups)], np.int32)
    seq_at = plan.seq ^ (member_seq[:, None] | sender[None, :])
    tp_at = plan.tp ^ member_tp
    position = (
        (seq_at * block_len)[:, :, None]
        + (tp_at * quarter)[:, None, None]
        + np.arange(quarter, dtype=np.int32)[None, None, :]
    )
    lens = lax.dynamic_slice_in_dim(lengths, plan.group * rows, rows, 0)

    def over_masks(array, masks, axis="seq"):
        sums = [0]
        for mask in masks:
            sums = sums + [m | mask for m in sums]
        return [swap(array, axis, m) for m in sums[1:]]

    def total_of(array, got):
        for other in got:
            array = array + other
        return array

    lane_block = lax.broadcasted_iota(jnp.int32, (4, width), 1) // norm_params.shape[1]
    small = jnp.where(lane_block == plan.seq, jnp.tile(norm_params.astype(bf16), (1, plan.n_seq)), 0)
    slim = entry_bias.shape[2]
    slot = lax.broadcasted_iota(jnp.int32, (slim, HD), 1) == plan.seq * slim + lax.broadcasted_iota(
        jnp.int32, (slim, HD), 0
    )
    placed = jnp.dot(entry_bias.reshape(-1, slim).astype(bf16), slot.astype(bf16), preferred_element_type=f32)
    placed = placed.astype(bf16).reshape(1, 3 * tp_width)
    placed = jnp.pad(placed, ((0, 0), (0, width - 3 * tp_width)))
    small = jnp.concatenate([small, placed], 0)
    seq_masks = [1 << i for i in range(plan.n_seq.bit_length() - 1)]
    last_mask = plan.outer[-1]
    first_masks = [m for m in seq_masks if m != last_mask]

    def columns(array, h, size):
        return array[..., h * size : (h + 1) * size].astype(bf16).reshape(array.shape[0], -1)

    def turned_columns(array, h):
        return array[:, h * hidden : (h + 1) * hidden].astype(bf16).T

    attn_mine = pick(
        [
            jnp.concatenate(
                [columns(entry_weight, h, head_width), columns(output_weight, h, head_width)], 1
            )
            for h in range(parts)
        ],
        plan.part_flags,
    )
    attn_block = plan.spread_mine(attn_mine, 0)
    resid = plan.over_groups(plan.outgoing_rows(inputs))
    attn_block, resid, small, gate_weight, down_weight, cotangent, position = hold(
        attn_block, resid, small, gate_weight, down_weight, cotangent, position
    )

    w_attn = plan.all_blocks(attn_block)
    small_got = over_masks(small, first_masks)
    gate_mine = pick([columns(gate_weight, h, hidden) for h in range(parts)], plan.part_flags)
    gate_block = plan.spread_mine(gate_mine, 0)
    small, small_got, resid, gate_block, cotangent, down_weight, position = hold(
        small, small_got, resid, gate_block, cotangent, down_weight, position
    )

    small = total_of(small, small_got)
    small_got = over_masks(small, [last_mask])
    down_mine = pick([columns(down_weight, h, hidden) for h in range(parts)], plan.part_flags)
    down_block = plan.spread_mine(down_mine, 0)
    small, small_got, down_block, gate_block, cotangent = hold(
        small, small_got, down_block, gate_block, cotangent
    )

    small = total_of(small, small_got)
    gains = plan.arranged(small[:4]).astype(f32)
    resid = plan.arranged(jnp.concatenate(resid, 0)).astype(f32)
    h_first, n_first, i_first = layer_norm(resid, gains[0], gains[1])
    low_first = h_first.astype(bf16)
    sides = plan.chips_sides(low_first)
    row_position = position.reshape(length)
    tables = turning(row_position) + (row_position[:, None], row_position[None, :])
    blank = jnp.zeros((down_block.shape[0], -(2 * hidden + hidden) % 128), bf16)
    ffn_block = jnp.concatenate([gate_block, down_block, blank], 1)
    low_first, sides, tables, ffn_block, cotangent = hold(low_first, sides, tables, ffn_block, cotangent)
    corner = plan.chips_corner(low_first, sides)
    outgoing = plan.outgoing_rows(cotangent)
    low_first, sides, corner, outgoing = hold(low_first, sides, corner, outgoing)
    near = plan.chips_near(low_first, sides, corner)
    other = plan.swap_core(near)
    a_first = jnp.concatenate([near, other], 0)
    a_first, w_attn, ffn_block, outgoing = hold(a_first, w_attn, ffn_block, outgoing)
    w_ffn = plan.all_blocks(ffn_block)
    grad_y = plan.over_groups(outgoing)
    own_position = jnp.broadcast_to(position[0][:, None, :], (groups, rows, quarter))
    real = (own_position < lens[None, :, None]).reshape(share, 1)

    w_entry = w_attn[:, : 3 * head_width]
    w_output = w_attn[:, 3 * head_width :]
    mixed = jnp.einsum("td,df->tf", a_first, w_entry, preferred_element_type=f32)
    mixed = mixed.reshape(plan.members * groups, rows, quarter, 3 * head_width)
    biases = [
        jnp.concatenate(
            [
                small[4:, c * tp_width + h * head_width : c * tp_width + (h + 1) * head_width]
                for c in range(3)
            ],
            1,
        )
        for h in range(parts)
    ]
    entry_shift = pick(biases, plan.part_flags)[0].astype(f32)
    qkv, att_low, attended, score_sums = attend_forward(mixed, entry_shift, tables, lens)
    att_low = att_low.reshape(plan.total, head_width)

    def output_product(lo, hi):
        return jnp.einsum("th,dh->td", att_low[lo:hi], w_output, preferred_element_type=f32)

    half = plan.total // 2
    far_product = output_product(half, plan.total).astype(bf16)
    far_product, grad_y = hold(far_product, grad_y)

    got = plan.swap_core(far_product)
    product = output_product(0, half)
    grad_y = plan.arranged(jnp.concatenate(grad_y, 0))
    grad_y = jnp.where(real, grad_y, 0)
    product, got, grad_y = hold(product, got, grad_y)

    near = (product, got)
    corner = plan.sum_corner(near)
    y_sides = plan.chips_sides(grad_y)
    near, corner, y_sides = hold(near, corner, y_sides)
    sides = plan.sum_sides(near, corner)
    y_corner = plan.chips_corner(grad_y, y_sides)
    near, sides, y_corner = hold(near, sides, y_corner)

    second = resid + plan.sum_end(near, sides)
    h_second, n_second, i_second = layer_norm(second, gains[2], gains[3])
    low_second = h_second.astype(bf16)
    sides = plan.chips_sides(low_second)
    y_near = plan.chips_near(grad_y, y_sides, y_corner)
    y_other = plan.swap_core(y_near)
    second, low_second, sides, y_near, y_other = hold(second, low_second, sides, y_near, y_other)
    corner = plan.chips_corner(low_second, sides)
    grad_y_all = jnp.concatenate([y_near, y_other], 0)
    low_second, sides, corner, grad_y_all = hold(low_second, sides, corner, grad_y_all)
    near = plan.chips_near(low_second, sides, corner)
    other = plan.swap_core(near)
    a_second = jnp.concatenate([near, other], 0)
    a_second, w_ffn = hold(a_second, w_ffn)

    w_gate = w_ffn[:, : 2 * hidden]
    gated = jnp.einsum("td,df->tf", a_second, w_gate, preferred_element_type=f32)
    gate = gated[:, :hidden]
    upper = gated[:, hidden:]
    sigma = jax.nn.sigmoid(gate)
    active_gate = gate * sigma
    hid = (active_gate * upper).astype(bf16)
    grad_down = jnp.einsum("td,tf->df", grad_y_all, hid, preferred_element_type=f32).astype(bf16)
    hid, grad_down, w_ffn = hold(hid, grad_down, w_ffn)
    w_down = w_ffn[:, 2 * hidden : 3 * hidden]
    down_sum = plan.sum_blocks(grad_down)
    grad_hidden = jnp.einsum(
        "td,df->tf", grad_y_all, w_down, preferred_element_type=f32
    ).astype(bf16)
    grad_gate_val = grad_hidden * upper * (sigma * (1.0 + gate * (1.0 - sigma)))
    grad_up_val = grad_hidden * active_gate
    grad_gated = jnp.concatenate([grad_gate_val, grad_up_val], 1).astype(bf16)

    def gate_product(lo, hi):
        return jnp.einsum("tf,df->td", grad_gated[lo:hi], w_gate, preferred_element_type=f32)

    def down_product(lo, hi):
        return jnp.einsum("tf,df->td", hid[lo:hi], w_down, preferred_element_type=f32)

    far_product = gate_product(half, plan.total).astype(bf16)
    hid, grad_gated, far_product = hold(hid, grad_gated, far_product)

    got = plan.swap_core(far_product)
    product = gate_product(0, half)
    grad_gate = jnp.einsum("td,tf->df", a_second, grad_gated, preferred_element_type=f32).astype(bf16)
    product, got, hid, grad_gate, down_sum = hold(product, got, hid, grad_gate, down_sum)
    gate_sum = plan.sum_blocks(grad_gate)

    near = (product, got)
    corner = plan.sum_corner(near)
    near, corner, hid, down_sum = hold(near, corner, hid, down_sum)
    sides = plan.sum_sides(near, corner)
    out_far = down_product(half, plan.total).astype(bf16)
    near, sides, out_far, hid, down_sum = hold(near, sides, out_far, hid, down_sum)

    out_got = plan.swap_core(out_far)
    grad_h2 = plan.sum_end(near, sides)
    grad_second = grad_y.astype(f32) + norm_back(grad_h2, n_second, i_second, gains[2])
    low_grad = grad_second.astype(bf16)
    sides = plan.chips_sides(low_grad)
    out_near = down_product(0, half)
    low_grad, sides, out_near, out_got, grad_h2, grad_second = hold(
        low_grad, sides, out_near, out_got, grad_h2, grad_second
    )
    out_near = (out_near, out_got)
    corner = plan.chips_corner(low_grad, sides)
    out_corner = plan.sum_corner(out_near)
    low_grad, sides, corner, out_corner, out_near = hold(low_grad, sides, corner, out_corner, out_near)

    near = plan.chips_near(low_grad, sides, corner)
    other = plan.swap_core(near)
    near, other = hold(near, other)
    grad_second_all = jnp.concatenate([near, other], 0)
    grad_att = jnp.einsum(
        "td,dh->th", grad_second_all, w_output, preferred_element_type=f32
    ).astype(bf16)
    grad_att = grad_att.reshape(attended.shape)
    grad_mixed, bias_sum = attend_backward(qkv, grad_att, attended, score_sums, tables, lens)
    grad_mixed = grad_mixed.reshape(plan.total, 3 * head_width)

    def entry_product(lo, hi):
        return jnp.einsum("tf,df->td", grad_mixed[lo:hi], w_entry, preferred_element_type=f32)

    far_product = entry_product(half, plan.total).astype(bf16)
    out_sides = plan.sum_sides(out_near, out_corner)
    far_product, grad_mixed, bias_sum, out_sides, out_near = hold(
        far_product, grad_mixed, bias_sum, out_sides, out_near
    )

    got = plan.swap_core(far_product)
    product = entry_product(0, half)
    grad_attn = jnp.concatenate(
        [
            jnp.einsum("td,tf->df", a_first, grad_mixed, preferred_element_type=f32).astype(bf16),
            jnp.einsum("td,tf->df", grad_second_all, att_low, preferred_element_type=f32).astype(bf16),
        ],
        1,
    )
    bias_sum = jnp.sum(bias_sum[:, 0], 0, keepdims=True)
    bias_got = over_masks(bias_sum, plan.outer)
    result = second + plan.sum_end(out_near, out_sides)
    out_returning = plan.returning_rows(result.astype(bf16))
    product, got, grad_attn, bias_sum, bias_got, down_sum, out_returning, gate_sum = hold(
        product, got, grad_attn, bias_sum, bias_got, down_sum, out_returning, gate_sum
    )
    attn_sum = plan.sum_blocks(grad_attn)

    bias_sum = total_of(bias_sum, bias_got)
    near = (product, got)
    corner = plan.sum_corner(near)
    bias_got = [swap(bias_sum, "seq", plan.inner_mask(j)) for j in range(1, parts)]
    near, corner, bias_sum, bias_got, down_sum, gate_sum, out_returning = hold(
        near, corner, bias_sum, bias_got, down_sum, gate_sum, out_returning
    )
    out_back = plan.over_groups(out_returning)
    sides = plan.sum_sides(near, corner)
    near, sides, out_back, down_sum, gate_sum = hold(near, sides, out_back, down_sum, gate_sum)

    def ordered_as(grad, *order):
        return with_layout_constraint(grad, Layout(order))

    beta = min(0.999, (1 + STEP) / (10 + STEP))

    def stepped(index, grad, master, moment, average):
        grad = grad + decays[index] * master
        moment = 0.9 * moment + grad
        weight = master - rates[index] * (grad + 0.9 * moment)
        return moment, weight, beta * average + (1.0 - beta) * weight, weight.astype(bf16)

    def along_tp(own):
        return gather(own, [("tp", m, m) for m in plan.tp_masks[:0:-1]])

    out_pieces = along_tp(plan.returned_rows(out_back, quarter, inputs.shape[1]))
    grad_h1 = plan.sum_end(near, sides)
    grad_input = grad_second + norm_back(grad_h1, n_first, i_first, gains[0])
    back = plan.over_groups(plan.returning_rows(grad_input.astype(bf16)))
    grad_gate = plan.collect_home(gate_sum)
    grad_down = plan.collect_home(down_sum)
    sums = jnp.stack(
        [
            jnp.sum(grad_h1 * n_first, 0),
            jnp.sum(grad_h1, 0),
            jnp.sum(grad_h2 * n_second, 0),
            jnp.sum(grad_h2, 0),
        ]
    )
    sums_got = over_masks(sums, plan.outer)
    back, grad_gate, grad_down, sums, sums_got, out_pieces = hold(
        back, grad_gate, grad_down, sums, sums_got, out_pieces
    )

    pieces = along_tp(plan.returned_rows(back, quarter, inputs.shape[1]))
    sums = total_of(sums, sums_got)
    sums_got = over_masks(sums, plan.tp_masks, "tp")
    pieces, out_pieces, sums, sums_got, grad_gate, grad_down, attn_sum = hold(
        pieces, out_pieces, sums, sums_got, grad_gate, grad_down, attn_sum
    )

    grad_gate = ordered_as(
        joined([part.reshape(part.shape[0], 2, hidden) for part in grad_gate], -1), 0, 1, 2
    )
    gate = stepped(4, grad_gate, gate_master, moment_gate, average_gate)
    grad_down = ordered_as(joined(grad_down, -1), 0, 1)
    down = stepped(5, grad_down, down_master, moment_down, average_down)
    attn_home = plan.collect_home(attn_sum)
    sums = plan.restored(total_of(sums, sums_got))
    sums_got = over_masks(sums, plan.inner)
    keys = sorted(pieces)
    core = plan.tp_masks[0]
    near = joined([pieces[k] for k in keys] + [out_pieces[k] for k in keys])
    other = swap(near, "tp", core)
    attn_home, sums, sums_got, near, other, gate, down = hold(
        attn_home, sums, sums_got, near, other, gate, down
    )

    sums = total_of(sums, sums_got)
    size = pieces[0].shape[0]
    whole = []
    for part in range(2):
        at = part * len(keys)
        found = {k: near[(at + i) * size : (at + i + 1) * size] for i, k in enumerate(keys)}
        found.update({k | core: other[(at + i) * size : (at + i + 1) * size] for i, k in enumerate(keys)})
        whole.append(plan.of_tp(found).reshape(inputs.shape))
    input_grad, layer_out = whole

    got = [part.reshape(3, heads_here, HD) for part in [bias_sum] + bias_got]
    bias_sum = joined(pick(got, plan.part_flags), 1)
    grad_bias = lax.dynamic_slice_in_dim(bias_sum, plan.seq * slim, slim, 2)
    slim = norm_params.shape[1]
    grad_norm = lax.dynamic_slice_in_dim(sums, plan.seq * slim, slim, 1)

    norm = stepped(0, grad_norm, norm_params, moment_norm, average_norm)
    bias = stepped(2, grad_bias, entry_bias, moment_bias, average_bias)

    def turned_over(array):
        return jnp.swapaxes(array, 0, 1)

    grad_entry = jnp.stack(
        [
            joined([part[:, c * head_width : (c + 1) * head_width] for part in attn_home], -1)
            for c in range(3)
        ]
    )
    grad_output = ordered_as(joined([part[:, 3 * head_width :] for part in attn_home], -1), 0, 1)
    entry = stepped(
        1, grad_entry, turned_over(entry_weight), turned_over(moment_entry), turned_over(average_entry)
    )
    entry = [turned_over(array) for array in entry]
    output = stepped(3, grad_output, output_weight, moment_output, average_output)
    kinds = zip(norm, entry, bias, output, gate, down)
    return (layer_out, input_grad, *(array for kind in kinds for array in kind))


def solution(mesh):
    in_specs = (
        P("seq", None, None),
        P("seq", None, None),
        P(),
        P(None, "seq"),
        P("seq", None, "tp"),
        P(None, "tp", "seq"),
        P("seq", "tp"),
        P("seq", None, "tp"),
        P("seq", "tp"),
        P(None, "seq"),
        P("seq", None, "tp"),
        P(None, "tp", "seq"),
        P("seq", "tp"),
        P("seq", None, "tp"),
        P("seq", "tp"),
        P(None, "seq"),
        P("seq", None, "tp"),
        P(None, "tp", "seq"),
        P("seq", "tp"),
        P("seq", None, "tp"),
        P("seq", "tp"),
    )
    out_specs = (
        P("seq", None, None),
        P("seq", None, None),
        P(None, "seq"),
        P("seq", None, "tp"),
        P(None, "tp", "seq"),
        P("seq", "tp"),
        P("seq", None, "tp"),
        P("seq", "tp"),
        P(None, "seq"),
        P("seq", None, "tp"),
        P(None, "tp", "seq"),
        P("seq", "tp"),
        P("seq", None, "tp"),
        P("seq", "tp"),
        P(None, "seq"),
        P("seq", None, "tp"),
        P(None, "tp", "seq"),
        P("seq", "tp"),
        P("seq", None, "tp"),
        P("seq", "tp"),
        P(None, "seq"),
        P("seq", None, "tp"),
        P(None, "tp", "seq"),
        P("seq", "tp"),
        P("seq", None, "tp"),
        P("seq", "tp"),
    )
    return jax.shard_map(body, mesh=mesh, in_specs=in_specs, out_specs=out_specs, check_vma=False)
```
